256 devices in a mesh: dp: 8 (over x, core), seq: 32 (over y, z).
Axes of the slice: x: 4, y: 4, z: 8, core: 2. Of those that a mesh axis runs over, the one named last changes fastest.
Arguments:
- node_queries: bfloat16 [8, 4096, 1024], P('dp', 'seq'), may hold values from -6 to 6
- node_keys: bfloat16 [8, 4096, 1024], P('dp', 'seq'), may hold values from -6 to 6
- node_values: bfloat16 [8, 4096, 1024], P('dp', 'seq'), may hold values from -6 to 6
- cotangent: bfloat16 [8, 4096, 1024], P('dp', 'seq'), may hold values from -6 to 6
- w_out: bfloat16 [1024, 1024], replicated, may hold values from -0.1875 to 0.1875
- neighbours: int32 [8, 32, 4], P('dp'), may hold values from -1 to 31, as said below
- contacts: int32 [8, 32, 8], P('dp'), may hold values from -1 to 31, as said below
- ownership: int32 [8, 32], P('dp'), may hold values from 0 to 3, never falling along the last dimension, each value on 1 to 16 neighbouring positions
Outputs:
- output: bfloat16 [8, 4096, 1024], P('dp', 'seq')
- query_gradient: bfloat16 [8, 4096, 1024], P('dp', 'seq')
- key_grad: bfloat16 [8, 4096, 1024], P('dp', 'seq')
- value_grad: bfloat16 [8, 4096, 1024], P('dp', 'seq')
- weight_grad: float32 [1024, 1024], P('seq')
The draws below stay inside these ranges and needn't reach their ends.
Inputs may be any that keep to these rules, and one draw needn't show every extreme that they name: `neighbours`: entry n of block b's row is b + o with o = -2, -1, 1, 2 for n = 0, 1, 2, 3, or -1; it is -1 where b + o lies outside the scene, and in some other slots. `contacts`: in each row the live entries come first and the rest are -1; live entries are distinct blocks that lie more than 2 blocks away from the row's own block. `ownership`: ownership never falls from one block to the next.
All inputs are finite; a program needn't handle non-finite values.
Results may differ from the reference program's by a relative error of at most 0.015.
Values may be sent and summed in bfloat16 or wider, within the bound.
A program may use at most 64 MiB of HBM per device.

```python
import math
import jax
import jax.numpy as jnp
import numpy as np
from jax import lax

D = 1024
HEADS = 16
HDIM = 64
FEAT = 1024
BLK = 128
NEIGH = 4
CONT = 8
PARTS_SIZE = 4
NBLOCKS = 32
NODES = 4096
SCENES = 8


def draw_node_queries(key, part):
    key = jax.random.fold_in(key, 11)
    value_key = jax.random.fold_in(key, 0)
    samples = jnp.clip(2.5 * jax.random.normal(value_key, (SCENES, NODES, FEAT)), -6.0, 6.0)
    return samples.astype(jnp.bfloat16)


def draw_node_keys(key, part):
    key = jax.random.fold_in(key, 13)
    value_key = jax.random.fold_in(key, 0)
    samples = jnp.clip(jax.random.normal(value_key, (SCENES, NODES, FEAT)), -6.0, 6.0)
    return samples.astype(jnp.bfloat16)


def draw_neighbours(key, part):
    key = jax.random.fold_in(key, 3)
    offsets = jnp.array([-2, -1, 1, 2], dtype=jnp.int32)
    targets = jnp.arange(NBLOCKS, dtype=jnp.int32)[:, None] + offsets[None, :]
    inside = (targets >= 0) & (targets < NBLOCKS)
    active = jax.random.randint(key, (SCENES, NBLOCKS, NEIGH), 0, 4) > 0
    return jnp.where(active & inside[None], targets[None], -1).astype(jnp.int32)


def draw_contacts(key, part):
    key = jax.random.fold_in(key, 5)
    rank_key, amount_key = jax.random.split(key)
    block_ids = jnp.arange(NBLOCKS, dtype=jnp.int32)
    rank_scores = jax.random.randint(rank_key, (SCENES, NBLOCKS, NBLOCKS), 0, 4096) * NBLOCKS + block_ids[None, None, :]
    nearby = jnp.abs(block_ids[:, None] - block_ids[None, :]) <= 2
    rank_scores = jnp.where(nearby[None], -1, rank_scores)
    _, chosen = lax.top_k(rank_scores, CONT)
    amounts = jax.random.randint(amount_key, (SCENES, NBLOCKS, 1), 0, CONT + 1)
    slot_index = jnp.arange(CONT, dtype=jnp.int32)
    return jnp.where(slot_index[None, None, :] < amounts, chosen, -1).astype(jnp.int32)


def block_scale(stream_key, shape, pieces, smallest, high):
    def one(dim, parts):
        steps = jax.random.uniform(jax.random.fold_in(jax.random.fold_in(stream_key, 6), dim), (parts,), jnp.float32, smallest / len(pieces), high / len(pieces))
        return jnp.repeat(jnp.exp(steps), shape[dim] // parts).reshape((-1,) + (1,) * (len(shape) - dim - 1))

    loudness = one(*pieces[0])
    for cut in pieces[1:]:
        loudness = loudness * one(*cut)
    return loudness


def length_profile(amount, total, bound, slope):
    loads = [(1 << 20) // math.isqrt(grade ** slope) + 1 for grade in range(2, amount + 1)]
    rest, given = total - bound - (amount - 1), [1] * (amount - 1)
    while rest > 0:
        candidates = [i for i in range(amount - 1) if given[i] < bound]
        whole, left = sum([loads[i] for i in candidates]), rest
        for i in candidates:
            extra = min(bound - given[i], max(1, left * loads[i] // whole), rest)
            given[i] = given[i] + extra
            rest = rest - extra
    return np.array([bound] + given)


def ragged(rng, number_of, total, reach, lean):
    if number_of == 2:
        one = jax.random.randint(rng, (), max(1, total - reach), min(reach, total - 1) + 1)
        return jnp.stack([one, total - one])
    lengths = jnp.asarray(length_profile(number_of, total, reach, lean), jnp.int32)
    twos = (number_of - 1) // 2
    source_of, taker = lengths[1:1 + 2 * twos:2], lengths[2:2 + 2 * twos:2]
    room = jnp.minimum(source_of - 1, reach - taker)
    moved = jax.random.randint(jax.random.fold_in(rng, 1), (twos,), 0, 1 << 20) % (room + 1)
    lengths = lengths.at[1:1 + 2 * twos:2].set(source_of - moved).at[2:2 + 2 * twos:2].set(taker + moved)
    return lengths[jax.random.permutation(jax.random.fold_in(rng, 2), number_of)]


def scatter_about(rng, shape, width, limit, shards=(), kind=jnp.bfloat16):
    level = block_scale(rng, shape, shards, -0.22, 0.18) if shards else 1.0
    result = jax.random.normal(rng, shape, jnp.float32) * width * level
    return jnp.minimum(jnp.maximum(result, -limit), limit).astype(kind)


def setup_inputs(seed: int = 0) -> dict:
    seeds = jax.random.split(jax.random.key(seed), 9)
    return {
        "node_queries": draw_node_queries(jax.random.fold_in(seeds[8], 71), 0),
        "node_keys": draw_node_keys(jax.random.fold_in(seeds[8], 71), 0),
        "node_values": scatter_about(seeds[2], (SCENES, NODES, FEAT), 1.0, 6.0, ((0, 8), (1, 32))),
        "cotangent": scatter_about(seeds[3], (SCENES, NODES, D), 1.0, 6.0, ((0, 8), (1, 32))),
        "w_out": scatter_about(seeds[4], (FEAT, D), FEAT ** -0.5, 0.1875),
        "neighbours": draw_neighbours(jax.random.fold_in(seeds[8], 71), 0),
        "contacts": draw_contacts(jax.random.fold_in(seeds[8], 71), 0),
        "ownership": jax.vmap(lambda own: jnp.searchsorted(jnp.cumsum(ragged(own, PARTS_SIZE, NBLOCKS, NBLOCKS // 2, 0)), jnp.arange(NBLOCKS), side="right"))(jax.random.split(seeds[7], SCENES)).reshape((SCENES, NBLOCKS)).astype(jnp.int32),
    }


def rounded_output(matrix):
    return lax.optimization_barrier(matrix.astype(jnp.bfloat16))


def block_table(neighbours, contacts, ownership):
    block_count = neighbours.shape[0]
    block_ids = jnp.arange(block_count, dtype=jnp.int32)
    matches = contacts[:, :, None] == block_ids[None, None, :]
    shared = jnp.any(matches & (ownership[None, None, :] == ownership[:, None, None]), axis=-1)
    slot_table = jnp.concatenate([block_ids[:, None], neighbours, contacts], axis=1)
    slot_valid = jnp.concatenate(
        [jnp.ones((block_count, 1), dtype=bool), neighbours >= 0, (contacts >= 0) & jnp.logical_not(shared)], axis=1)
    return jnp.maximum(slot_table, 0).astype(jnp.int32), slot_valid


def head_pass(head_arrays, slot_table, slot_valid):
    query_head, key_head, value_head, grad_head = head_arrays
    selected_key_rows = key_head[slot_table].astype(jnp.float32)
    selected_value_rows = value_head[slot_table].astype(jnp.float32)
    query_wide_float = query_head.astype(jnp.float32)
    gradient_wide_float = grad_head.astype(jnp.float32)
    logit_scores = jnp.einsum("gye,gwte->gywt", query_wide_float, selected_key_rows) * 0.125
    logit_scores = jnp.where(slot_valid[:, None, :, None], logit_scores, -jnp.inf)
    row_max = jnp.max(logit_scores, axis=(2, 3), keepdims=True)
    log_total = row_max + jnp.log(jnp.sum(jnp.exp(logit_scores - row_max), axis=(2, 3), keepdims=True))
    probabilities = jnp.exp(logit_scores - log_total)
    softmax_weights = rounded_output(probabilities).astype(jnp.float32)
    attention_result = rounded_output(jnp.einsum("fhcp,fcpm->fhm", softmax_weights, selected_value_rows))
    row_delta = jnp.sum(gradient_wide_float * attention_result.astype(jnp.float32), axis=-1)
    probability_gradient = jnp.einsum("gye,gwte->gywt", gradient_wide_float, selected_value_rows)
    score_gradient = rounded_output(probabilities * (probability_gradient - row_delta[:, :, None, None])).astype(jnp.float32)
    query_gradient = (jnp.einsum("fhcp,fcpm->fhm", score_gradient, selected_key_rows) * 0.125).astype(jnp.bfloat16)
    key_products = jnp.einsum("peio,per->pior", score_gradient, query_wide_float) * 0.125
    value_products = jnp.einsum("peio,per->pior", softmax_weights, gradient_wide_float)
    zero_blocks = jnp.zeros(key_head.shape, jnp.float32)
    key_grad = zero_blocks.at[slot_table].add(key_products).astype(jnp.bfloat16)
    value_grad = zero_blocks.at[slot_table].add(value_products).astype(jnp.bfloat16)
    return attention_result, query_gradient, key_grad, value_grad


def reference(node_queries, node_keys, node_values, cotangent, w_out, neighbours, contacts, ownership):
    def split_heads(matrix):
        return matrix.reshape(NBLOCKS, BLK, HEADS, HDIM).transpose(2, 0, 1, 3)

    def join_heads(stacked):
        return stacked.transpose(1, 2, 0, 3).reshape(NODES, FEAT)

    def one_scene(scene_arrays):
        queries, keys_in, values_in, grad_out, neighbour_rows, contact_rows, owner_row = scene_arrays
        slot_table, slot_valid = block_table(neighbour_rows, contact_rows, owner_row)
        attention_grad = rounded_output(jnp.dot(grad_out, w_out.T, preferred_element_type=jnp.float32))
        results = lax.map(lambda head_arrays: head_pass(head_arrays, slot_table, slot_valid),
                          (split_heads(queries), split_heads(keys_in), split_heads(values_in),
                           split_heads(attention_grad)))
        attention_result, query_gradient, key_grad, value_grad = [join_heads(stacked) for stacked in results]
        output = jnp.dot(attention_result, w_out, preferred_element_type=jnp.float32).astype(jnp.bfloat16)
        weight_part = jnp.dot(attention_result.T, grad_out, preferred_element_type=jnp.float32)
        return output, query_gradient, key_grad, value_grad, weight_part

    output, query_gradient, key_grad, value_grad, weight_parts = lax.map(
        one_scene, (node_queries, node_keys, node_values, cotangent, neighbours, contacts, ownership))
    weight_grad = jnp.sum(weight_parts, axis=0) * (SCENES * NODES) ** -0.5
    return output, query_gradient, key_grad, value_grad, weight_grad
```

```python
import functools

import jax
import jax.numpy as jnp
from jax import lax
from jax.experimental import pallas as pl
from jax.experimental.pallas import tpu as pltpu
from jax.sharding import PartitionSpec as P

HEADS = 16
HDIM = 64
BLK = 128
NB = 32
HALF = 16
GROUP = 2
SLOTS = 16
MESH = pl.DeviceIdType.MESH
VMEM = pltpu.VMEM
BF = jnp.bfloat16
F32 = jnp.float32


def place():
    dp = lax.axis_index("dp")
    s = lax.axis_index("seq")
    return dp // 2, dp % 2, s


def partner(x, c, s, j):
    return (x * 2 + s % 2, 2 * j + c)


def greet(x, c, s):
    barrier = pltpu.get_barrier_semaphore()
    alone = c == s % 2

    @pl.loop(0, HALF)
    def _(j):
        @pl.when(jnp.logical_not(jnp.logical_and(alone, j == s // 2)))
        def _():
            pl.semaphore_signal(barrier, inc=1, device_id=partner(x, c, s, j), device_id_type=MESH)

    pl.semaphore_signal(barrier, inc=1, device_id=(x * 2 + 1 - c, s), device_id_type=MESH)
    pl.semaphore_wait(barrier, jnp.where(alone, HALF, HALF + 1))


def scatter_kernel(
    q_ref, k_ref, v_ref, cot_ref, w_ref, tab_ref,
    kv_ref, qd_ref, tabo_ref,
    send_kv, send_qd, tab_sib,
    kv_ss, kv_rs, qd_ss, qd_rs, re_ss, re_rs, tb_ss, tb_rs,
):
    x, c, s = place()
    alone = c == s % 2
    mine = s // 2
    sibling = (x * 2 + 1 - c, s)
    greet(x, c, s)

    def is_self(j):
        return jnp.logical_and(alone, j == mine)

    tab_copy = pltpu.make_async_remote_copy(
        src_ref=tab_ref, dst_ref=tab_sib, send_sem=tb_ss, recv_sem=tb_rs,
        device_id=sibling, device_id_type=MESH)
    tab_copy.start()

    def kv_out(j):
        return pltpu.make_async_remote_copy(
            src_ref=send_kv.at[j], dst_ref=kv_ref.at[s], send_sem=kv_ss.at[j], recv_sem=kv_rs.at[mine],
            device_id=partner(x, c, s, j), device_id_type=MESH)

    def qd_out(j):
        return pltpu.make_async_remote_copy(
            src_ref=send_qd.at[j], dst_ref=qd_ref.at[mine], send_sem=qd_ss.at[j], recv_sem=qd_rs.at[mine],
            device_id=partner(x, c, s, j), device_id_type=MESH)

    def kv_in(j):
        return pltpu.make_async_remote_copy(
            src_ref=send_kv.at[j], dst_ref=kv_ref.at[2 * j + c], send_sem=kv_ss.at[j], recv_sem=kv_rs.at[j],
            device_id=partner(x, c, s, j), device_id_type=MESH)

    def qd_in(j):
        return pltpu.make_async_remote_copy(
            src_ref=send_qd.at[j], dst_ref=qd_ref.at[j], send_sem=qd_ss.at[j], recv_sem=qd_rs.at[j],
            device_id=partner(x, c, s, j), device_id_type=MESH)

    def relay(j, odd):
        return pltpu.make_async_remote_copy(
            src_ref=kv_ref.at[2 * j + odd], dst_ref=kv_ref.at[2 * j + odd], send_sem=re_ss.at[j], recv_sem=re_rs.at[j],
            device_id=sibling, device_id_type=MESH)

    @pl.loop(0, HEADS // 2)
    def _(t):
        pair = (t + s // 4) % (HEADS // 2)
        cols = pl.ds(pl.multiple_of(pair * 128, 128), 128)
        k = k_ref[:, cols]
        v = v_ref[:, cols]
        for e in range(2):
            j = pair * 2 + e
            send_kv[j] = jnp.concatenate([k[:, e * 64:e * 64 + 64], v[:, e * 64:e * 64 + 64]], axis=1)

            @pl.when(jnp.logical_not(is_self(j)))
            def _():
                kv_out(j).start()

            @pl.when(is_self(j))
            def _():
                kv_ref[s] = send_kv[j]

    @pl.loop(0, HEADS // 2)
    def _(t):
        pair = (t + s // 4) % (HEADS // 2)
        cols = pl.ds(pl.multiple_of(pair * 128, 128), 128)
        q = q_ref[:, cols] * jnp.asarray(0.125, BF)
        d = lax.dot_general(cot_ref[...], w_ref[cols, :], (((1,), (1,)), ((), ())),
                            preferred_element_type=F32).astype(BF)
        for e in range(2):
            j = pair * 2 + e
            send_qd[j] = jnp.concatenate([q[:, e * 64:e * 64 + 64], d[:, e * 64:e * 64 + 64]], axis=1)

            @pl.when(jnp.logical_not(is_self(j)))
            def _():
                qd_out(j).start()

            @pl.when(is_self(j))
            def _():
                qd_ref[mine] = send_qd[j]

    @pl.loop(0, HALF)
    def _(t):
        j = (t + mine) % HALF

        @pl.when(jnp.logical_not(is_self(j)))
        def _():
            kv_in(j).wait_recv()

        relay(j, c).start()

    tab_copy.wait()
    own = jnp.broadcast_to(alone.astype(jnp.int32), tab_ref.shape)
    tabo_ref[...] = tab_ref[...] * own + tab_sib[...] * (1 - own)

    @pl.loop(0, HALF)
    def _(t):
        j = (t + mine) % HALF
        relay(j, 1 - c).wait_recv()

        @pl.when(jnp.logical_not(is_self(j)))
        def _():
            qd_in(j).wait_recv()

    @pl.loop(0, HALF)
    def _(j):
        relay(j, c).wait_send()

        @pl.when(jnp.logical_not(is_self(j)))
        def _():
            kv_out(j).wait_send()
            qd_out(j).wait_send()


def core_kernel(tab_ref, kv_ref, qd_ref, par_ref, out_ref, dkv_ref, kvt, acc, sbuf, pbuf, qd2, qd2t, slots):
    c = par_ref[0]

    @pl.loop(0, NB)
    def _(b):
        kvt[b] = kv_ref[b].T
        acc[b] = jnp.zeros((BLK, BLK), F32)

    qd2[...] = jnp.zeros((2 * BLK, BLK), BF)
    qd2t[...] = jnp.zeros((BLK, 2 * BLK), BF)
    rows = GROUP * BLK

    @pl.loop(0, HALF)
    def _(i):
        b = 2 * i + c
        owner = tab_ref[b, 12]
        for e in range(SLOTS):
            slots[e] = b
        n = jnp.int32(1)
        for e in range(12):
            other = tab_ref[b, e]
            good = other >= 0
            if e >= 4:
                good = jnp.logical_and(good, tab_ref[jnp.maximum(other, 0), 12] != owner)
            slots[n] = jnp.where(good, other, b)
            n = n + good.astype(jnp.int32)
        steps = (n + GROUP - 1) // GROUP

        qd = qd_ref[i]
        qdt = qd.T
        qd2[0:BLK, 0:HDIM] = qd[:, 0:HDIM]
        qd2[BLK:, HDIM:] = qd[:, HDIM:]
        qd2t[0:HDIM, 0:BLK] = qdt[0:HDIM, :]
        qd2t[HDIM:, BLK:] = qdt[HDIM:, :]

        def scores(g, m):
            keys = jnp.concatenate([kv_ref[slots[g * GROUP + u]] for u in range(GROUP)], axis=0)
            both = jnp.dot(keys, qd2t[...], preferred_element_type=F32)
            for u in range(GROUP):
                bias = jnp.where(g * GROUP + u < n, 0.0, -jnp.inf).astype(F32)
                part = both[u * BLK:(u + 1) * BLK, 0:BLK] + bias
                sbuf[g * GROUP + u] = part
                pbuf[g * GROUP + u] = both[u * BLK:(u + 1) * BLK, BLK:]
                m = jnp.maximum(m, jnp.max(part.reshape(BLK // 8, 8, BLK), axis=0))
            return m

        m = lax.fori_loop(0, steps, scores, jnp.full((8, BLK), -jnp.inf, F32))
        m = jnp.broadcast_to(jnp.max(m, axis=0, keepdims=True), (8, BLK))

        def weigh(g, carry):
            total, dot = carry
            for u in range(GROUP):
                part = jnp.exp(sbuf[g * GROUP + u].reshape(BLK // 8, 8, BLK) - m[None])
                sbuf[g * GROUP + u] = part.reshape(BLK, BLK)
                total = total + jnp.sum(part, axis=0)
                dot = dot + jnp.sum(part * pbuf[g * GROUP + u].reshape(BLK // 8, 8, BLK), axis=0)
            return total, dot

        zero = jnp.zeros((8, BLK), F32)
        total, dot = lax.fori_loop(0, steps, weigh, (zero, zero))
        inv = 1.0 / jnp.sum(total, axis=0, keepdims=True)
        delta = jnp.broadcast_to(jnp.sum(dot, axis=0, keepdims=True) * inv, (8, BLK))
        inv = jnp.broadcast_to(inv, (8, BLK))

        def grads(g, carry):
            dq, at = carry
            parts = []
            for u in range(GROUP):
                prob = sbuf[g * GROUP + u].reshape(BLK // 8, 8, BLK) * inv[None]
                ds = prob * (pbuf[g * GROUP + u].reshape(BLK // 8, 8, BLK) - delta[None])
                parts.append(jnp.concatenate(
                    [ds.reshape(BLK, BLK).astype(BF), prob.reshape(BLK, BLK).astype(BF)], axis=1))
            both = jnp.concatenate(parts, axis=0)
            dkv = jnp.dot(both, qd2[...], preferred_element_type=F32)
            for u in range(GROUP):
                other = slots[g * GROUP + u]
                acc[other] = acc[other] + dkv[u * BLK:(u + 1) * BLK]
            keys = jnp.concatenate([kvt[slots[g * GROUP + u]] for u in range(GROUP)], axis=1)
            mixed = jnp.dot(keys, both, preferred_element_type=F32)
            return dq + mixed[0:HDIM, 0:BLK], at + mixed[HDIM:, BLK:]

        zero = jnp.zeros((HDIM, BLK), F32)
        dq, at = lax.fori_loop(0, steps, grads, (zero, zero))
        out_ref[i] = jnp.concatenate([dq * 0.125, at], axis=0).T.astype(BF)

    @pl.loop(0, HALF)
    def _(i):
        for e in range(2):
            dkv_ref[e, i] = acc[2 * i + e].astype(BF)


def gather_kernel(
    od_ref, dkv_ref, w_ref,
    o_ref, dq_ref, dk_ref, dv_ref, at_ref,
    ret_a, ret_b, sib, send_b,
    a_ss, a_rs, b_ss, b_rs, s_ss, s_rs,
):
    x, c, s = place()
    alone = c == s % 2
    mine = s // 2
    sibling = (x * 2 + 1 - c, s)
    greet(x, c, s)

    def is_self(j):
        return jnp.logical_and(alone, j == mine)

    def a_copy(j, slot):
        return pltpu.make_async_remote_copy(
            src_ref=od_ref.at[j], dst_ref=ret_a.at[slot], send_sem=a_ss.at[j], recv_sem=a_rs.at[slot],
            device_id=partner(x, c, s, j), device_id_type=MESH)

    def b_copy(j, slot):
        return pltpu.make_async_remote_copy(
            src_ref=send_b.at[j], dst_ref=ret_b.at[slot], send_sem=b_ss.at[j], recv_sem=b_rs.at[slot],
            device_id=partner(x, c, s, j), device_id_type=MESH)

    def s_copy(r):
        return pltpu.make_async_remote_copy(
            src_ref=dkv_ref.at[1 - c, pl.ds(r * 4, 4)], dst_ref=sib.at[pl.ds(r * 4, 4)],
            send_sem=s_ss.at[r], recv_sem=s_rs.at[r],
            device_id=sibling, device_id_type=MESH)

    @pl.loop(0, 4)
    def _(t):
        s_copy((t + s // 8) % 4).start()

    @pl.loop(0, HALF)
    def _(t):
        j = (t + mine) % HALF

        @pl.when(jnp.logical_not(is_self(j)))
        def _():
            a_copy(j, mine).start()

        @pl.when(is_self(j))
        def _():
            ret_a[mine] = od_ref[j]

    @pl.loop(0, 4)
    def _(t):
        r = (t + s // 8) % 4
        s_copy(r).wait_recv()

        @pl.loop(0, 4)
        def _(u):
            j = r * 4 + u
            send_b[j] = (dkv_ref[c, j].astype(F32) + sib[j].astype(F32)).astype(BF)

            @pl.when(jnp.logical_not(is_self(j)))
            def _():
                b_copy(j, mine).start()

            @pl.when(is_self(j))
            def _():
                ret_b[mine] = send_b[j]

    @pl.loop(0, HEADS // 2)
    def _(pair):
        cols = pl.ds(pl.multiple_of(pair * 128, 128), 128)
        for e in range(2):
            @pl.when(jnp.logical_not(is_self(pair * 2 + e)))
            def _():
                a_copy(pair * 2 + e, pair * 2 + e).wait_recv()

        a0 = ret_a[pair * 2]
        a1 = ret_a[pair * 2 + 1]
        dq_ref[:, cols] = jnp.concatenate([a0[:, 0:64], a1[:, 0:64]], axis=1)
        at_ref[:, cols] = jnp.concatenate([a0[:, 64:], a1[:, 64:]], axis=1)

    @pl.loop(0, 4)
    def _(t):
        cols = pl.ds(pl.multiple_of(t * 256, 256), 256)
        o_ref[:, cols] = jnp.dot(at_ref[...], w_ref[:, cols], preferred_element_type=F32).astype(BF)

    @pl.loop(0, HEADS // 2)
    def _(pair):
        cols = pl.ds(pl.multiple_of(pair * 128, 128), 128)
        for e in range(2):
            @pl.when(jnp.logical_not(is_self(pair * 2 + e)))
            def _():
                b_copy(pair * 2 + e, pair * 2 + e).wait_recv()

        a0 = ret_b[pair * 2]
        a1 = ret_b[pair * 2 + 1]
        dk_ref[:, cols] = jnp.concatenate([a0[:, 0:64], a1[:, 0:64]], axis=1)
        dv_ref[:, cols] = jnp.concatenate([a0[:, 64:], a1[:, 64:]], axis=1)

    @pl.loop(0, HALF)
    def _(j):
        @pl.when(jnp.logical_not(is_self(j)))
        def _():
            a_copy(j, mine).wait_send()
            b_copy(j, mine).wait_send()

    @pl.loop(0, 4)
    def _(r):
        s_copy(r).wait_send()


def spec(n):
    return [pl.BlockSpec(memory_space=VMEM)] * n


def attend(tab, kv, qd, parity):
    tile = lambda n, t: jax.ShapeDtypeStruct((n, BLK, BLK), t)
    return pl.pallas_call(
        core_kernel,
        out_shape=(tile(HALF, BF), jax.ShapeDtypeStruct((2, HALF, BLK, BLK), BF)),
        in_specs=[pl.BlockSpec(memory_space=pltpu.SMEM)] + spec(2) + [pl.BlockSpec(memory_space=pltpu.SMEM)],
        out_specs=tuple(spec(2)),
        scratch_shapes=[
            VMEM((NB, BLK, BLK), BF), VMEM((NB, BLK, BLK), F32),
            VMEM((SLOTS, BLK, BLK), F32), VMEM((SLOTS, BLK, BLK), F32),
            VMEM((2 * BLK, BLK), BF), VMEM((BLK, 2 * BLK), BF),
            pltpu.SMEM((SLOTS,), jnp.int32),
        ],
        compiler_params=pltpu.CompilerParams(vmem_limit_bytes=32 * 2**20),
        name="attend",
    )(tab, kv, qd, parity)


def local(node_queries, node_keys, node_values, cotangent, w_out, neighbours, contacts, ownership):
    tile = lambda n, t: jax.ShapeDtypeStruct((n, BLK, BLK), t)
    flat = jax.ShapeDtypeStruct((BLK, HEADS * HDIM), BF)
    dma = pltpu.SemaphoreType.DMA
    table = jnp.concatenate([neighbours[0], contacts[0], ownership[0][:, None]], axis=1)
    table = jnp.pad(table, ((0, 0), (0, 128 - 13)))
    kv, qd, tab = pl.pallas_call(
        scatter_kernel,
        out_shape=(tile(NB, BF), tile(HALF, BF), jax.ShapeDtypeStruct((NB, 128), jnp.int32)),
        in_specs=spec(6),
        out_specs=tuple(spec(3)),
        scratch_shapes=[
            VMEM((HALF, BLK, BLK), BF), VMEM((HALF, BLK, BLK), BF), VMEM((NB, 128), jnp.int32),
            dma((HALF,)), dma((HALF,)), dma((HALF,)), dma((HALF,)), dma((HALF,)), dma((HALF,)), dma, dma,
        ],
        compiler_params=pltpu.CompilerParams(
            collective_id=0, has_side_effects=True, vmem_limit_bytes=32 * 2**20),
        name="scatter_heads",
    )(node_queries[0], node_keys[0], node_values[0], cotangent[0], w_out, table)

    parity = (lax.axis_index("dp") % 2).astype(jnp.int32).reshape(1)
    od, dkv = attend(tab, kv, qd, parity)

    output, dq, dk, dv, att = pl.pallas_call(
        gather_kernel,
        out_shape=(flat,) * 5,
        in_specs=spec(3),
        out_specs=tuple(spec(5)),
        scratch_shapes=[
            VMEM((HALF, BLK, BLK), BF), VMEM((HALF, BLK, BLK), BF), VMEM((HALF, BLK, BLK), BF), VMEM((HALF, BLK, BLK), BF),
            dma((HALF,)), dma((HALF,)), dma((HALF,)), dma((HALF,)), dma((4,)), dma((4,)),
        ],
        compiler_params=pltpu.CompilerParams(
            collective_id=1, has_side_effects=True, vmem_limit_bytes=32 * 2**20),
        name="gather_nodes",
    )(od, dkv, w_out)

    scenes = lax.axis_size("dp")
    cot_all = lax.all_gather(cotangent[0], "dp", axis=0, tiled=True)
    share = att.reshape(BLK, NB, scenes, NB // scenes)
    share = lax.all_to_all(share, "dp", split_axis=2, concat_axis=0, tiled=True)
    share = share.reshape(scenes * BLK, NB * (NB // scenes))
    part = lax.dot_general(share, cot_all, (((0,), (0,)), ((), ())), preferred_element_type=F32)
    part = lax.psum_scatter(part.reshape(NB, (NB // scenes) * 1024), "seq", scatter_dimension=0, tiled=True)
    weight_grad = lax.all_gather(part.reshape(NB // scenes, 1024), "dp", axis=0, tiled=True)
    weight_grad = weight_grad * (scenes * NB * BLK) ** (-0.5)
    return (output[None], dq[None], dk[None], dv[None], weight_grad)


def solution(mesh):
    placed = (
        P("dp", "seq", None), P("dp", "seq", None), P("dp", "seq", None), P("dp", "seq", None),
        P(), P("dp", None, None), P("dp", None, None), P("dp", None),
    )
    return jax.shard_map(
        local,
        mesh=mesh,
        in_specs=placed,
        out_specs=(
            P("dp", "seq", None), P("dp", "seq", None), P("dp", "seq", None), P("dp", "seq", None),
            P("seq", None),
        ),
        check_vma=False,
    )
```

```python
import functools

import jax
import jax.numpy as jnp
from jax import lax
from jax.experimental import pallas as pl
from jax.experimental.pallas import tpu as pltpu
from jax.sharding import PartitionSpec as P

HEADS = 16
HDIM = 64
BLK = 128
NB = 32
SCENES = 8
HALF = 16
GROUP = 2
SLOTS = 16
MESH = pl.DeviceIdType.MESH
VMEM = pltpu.VMEM
BF = jnp.bfloat16
F32 = jnp.float32


def place():
    dp = lax.axis_index("dp")
    s = lax.axis_index("seq")
    return dp // 2, dp % 2, s


def partner(x, c, s, j):
    return (x * 2 + s % 2, 2 * j + c)


def greet(x, c, s):
    barrier = pltpu.get_barrier_semaphore()
    alone = c == s % 2

    @pl.loop(0, HALF)
    def _(j):
        @pl.when(jnp.logical_not(jnp.logical_and(alone, j == s // 2)))
        def _():
            pl.semaphore_signal(barrier, inc=1, device_id=partner(x, c, s, j), device_id_type=MESH)

    pl.semaphore_signal(barrier, inc=1, device_id=(x * 2 + 1 - c, s), device_id_type=MESH)
    pl.semaphore_wait(barrier, jnp.where(alone, HALF, HALF + 1))


def scatter_kernel(
    q_ref, k_ref, v_ref, cot_ref, w_ref, tab_ref,
    kv_ref, qd_ref, tabo_ref,
    send_kv, send_qd, tab_sib,
    kv_ss, kv_rs, qd_ss, qd_rs, re_ss, re_rs, tb_ss, tb_rs,
):
    x, c, s = place()
    alone = c == s % 2
    mine = s // 2
    sibling = (x * 2 + 1 - c, s)
    greet(x, c, s)

    def is_self(j):
        return jnp.logical_and(alone, j == mine)

    tab_copy = pltpu.make_async_remote_copy(
        src_ref=tab_ref, dst_ref=tab_sib, send_sem=tb_ss, recv_sem=tb_rs,
        device_id=sibling, device_id_type=MESH)
    tab_copy.start()

    def kv_out(j):
        return pltpu.make_async_remote_copy(
            src_ref=send_kv.at[j], dst_ref=kv_ref.at[s], send_sem=kv_ss.at[j], recv_sem=kv_rs.at[mine],
            device_id=partner(x, c, s, j), device_id_type=MESH)

    def qd_out(j):
        return pltpu.make_async_remote_copy(
            src_ref=send_qd.at[j], dst_ref=qd_ref.at[mine], send_sem=qd_ss.at[j], recv_sem=qd_rs.at[mine],
            device_id=partner(x, c, s, j), device_id_type=MESH)

    def kv_in(j):
        return pltpu.make_async_remote_copy(
            src_ref=send_kv.at[j], dst_ref=kv_ref.at[2 * j + c], send_sem=kv_ss.at[j], recv_sem=kv_rs.at[j],
            device_id=partner(x, c, s, j), device_id_type=MESH)

    def qd_in(j):
        return pltpu.make_async_remote_copy(
            src_ref=send_qd.at[j], dst_ref=qd_ref.at[j], send_sem=qd_ss.at[j], recv_sem=qd_rs.at[j],
            device_id=partner(x, c, s, j), device_id_type=MESH)

    def relay(j, odd):
        return pltpu.make_async_remote_copy(
            src_ref=kv_ref.at[2 * j + odd], dst_ref=kv_ref.at[2 * j + odd], send_sem=re_ss.at[j], recv_sem=re_rs.at[j],
            device_id=sibling, device_id_type=MESH)

    @pl.loop(0, HEADS // 2)
    def _(t):
        pair = (t + s // 4) % (HEADS // 2)
        cols = pl.ds(pl.multiple_of(pair * 128, 128), 128)
        k = k_ref[:, cols]
        v = v_ref[:, cols]
        for e in range(2):
            j = pair * 2 + e
            send_kv[j] = jnp.concatenate([k[:, e * 64:e * 64 + 64], v[:, e * 64:e * 64 + 64]], axis=1)

            @pl.when(jnp.logical_not(is_self(j)))
            def _():
                kv_out(j).start()

            @pl.when(is_self(j))
            def _():
                kv_ref[s] = send_kv[j]

    @pl.loop(0, HEADS // 2)
    def _(t):
        pair = (t + s // 4) % (HEADS // 2)
        cols = pl.ds(pl.multiple_of(pair * 128, 128), 128)
        q = q_ref[:, cols] * jnp.asarray(0.125, BF)
        d = lax.dot_general(cot_ref[...], w_ref[cols, :], (((1,), (1,)), ((), ())),
                            preferred_element_type=F32).astype(BF)
        for e in range(2):
            j = pair * 2 + e
            send_qd[j] = jnp.concatenate([q[:, e * 64:e * 64 + 64], d[:, e * 64:e * 64 + 64]], axis=1)

            @pl.when(jnp.logical_not(is_self(j)))
            def _():
                qd_out(j).start()

            @pl.when(is_self(j))
            def _():
                qd_ref[mine] = send_qd[j]

    @pl.loop(0, HALF)
    def _(t):
        j = (t + mine) % HALF

        @pl.when(jnp.logical_not(is_self(j)))
        def _():
            kv_in(j).wait_recv()

        relay(j, c).start()

    tab_copy.wait()
    own = jnp.broadcast_to(alone.astype(jnp.int32), tab_ref.shape)
    tabo_ref[...] = tab_ref[...] * own + tab_sib[...] * (1 - own)

    @pl.loop(0, HALF)
    def _(t):
        j = (t + mine) % HALF
        relay(j, 1 - c).wait_recv()

        @pl.when(jnp.logical_not(is_self(j)))
        def _():
            qd_in(j).wait_recv()

    @pl.loop(0, HALF)
    def _(j):
        relay(j, c).wait_send()

        @pl.when(jnp.logical_not(is_self(j)))
        def _():
            kv_out(j).wait_send()
            qd_out(j).wait_send()


def core_kernel(tab_ref, kv_ref, qd_ref, par_ref, out_ref, dkv_ref, kvt, acc, sbuf, pbuf, qd2, qd2t, slots):
    c = par_ref[0]

    @pl.loop(0, NB)
    def _(b):
        kvt[b] = kv_ref[b].T
        acc[b] = jnp.zeros((BLK, BLK), F32)

    qd2[...] = jnp.zeros((2 * BLK, BLK), BF)
    qd2t[...] = jnp.zeros((BLK, 2 * BLK), BF)
    rows = GROUP * BLK

    @pl.loop(0, HALF)
    def _(i):
        b = 2 * i + c
        owner = tab_ref[b, 12]
        for e in range(SLOTS):
            slots[e] = b
        n = jnp.int32(1)
        for e in range(12):
            other = tab_ref[b, e]
            good = other >= 0
            if e >= 4:
                good = jnp.logical_and(good, tab_ref[jnp.maximum(other, 0), 12] != owner)
            slots[n] = jnp.where(good, other, b)
            n = n + good.astype(jnp.int32)
        steps = (n + GROUP - 1) // GROUP

        qd = qd_ref[i]
        qdt = qd.T
        qd2[0:BLK, 0:HDIM] = qd[:, 0:HDIM]
        qd2[BLK:, HDIM:] = qd[:, HDIM:]
        qd2t[0:HDIM, 0:BLK] = qdt[0:HDIM, :]
        qd2t[HDIM:, BLK:] = qdt[HDIM:, :]

        def scores(g, m):
            keys = jnp.concatenate([kv_ref[slots[g * GROUP + u]] for u in range(GROUP)], axis=0)
            both = jnp.dot(keys, qd2t[...], preferred_element_type=F32)
            for u in range(GROUP):
                bias = jnp.where(g * GROUP + u < n, 0.0, -jnp.inf).astype(F32)
                part = both[u * BLK:(u + 1) * BLK, 0:BLK] + bias
                sbuf[g * GROUP + u] = part
                pbuf[g * GROUP + u] = both[u * BLK:(u + 1) * BLK, BLK:]
                m = jnp.maximum(m, jnp.max(part.reshape(BLK // 8, 8, BLK), axis=0))
            return m

        m = lax.fori_loop(0, steps, scores, jnp.full((8, BLK), -jnp.inf, F32))
        m = jnp.broadcast_to(jnp.max(m, axis=0, keepdims=True), (8, BLK))

        def weigh(g, carry):
            total, dot = carry
            for u in range(GROUP):
                part = jnp.exp(sbuf[g * GROUP + u].reshape(BLK // 8, 8, BLK) - m[None])
                sbuf[g * GROUP + u] = part.reshape(BLK, BLK)
                total = total + jnp.sum(part, axis=0)
                dot = dot + jnp.sum(part * pbuf[g * GROUP + u].reshape(BLK // 8, 8, BLK), axis=0)
            return total, dot

        zero = jnp.zeros((8, BLK), F32)
        total, dot = lax.fori_loop(0, steps, weigh, (zero, zero))
        inv = 1.0 / jnp.sum(total, axis=0, keepdims=True)
        delta = jnp.broadcast_to(jnp.sum(dot, axis=0, keepdims=True) * inv, (8, BLK))
        inv = jnp.broadcast_to(inv, (8, BLK))

        def grads(g, carry):
            dq, at = carry
            parts = []
            for u in range(GROUP):
                prob = sbuf[g * GROUP + u].reshape(BLK // 8, 8, BLK) * inv[None]
                ds = prob * (pbuf[g * GROUP + u].reshape(BLK // 8, 8, BLK) - delta[None])
                parts.append(jnp.concatenate(
                    [ds.reshape(BLK, BLK).astype(BF), prob.reshape(BLK, BLK).astype(BF)], axis=1))
            both = jnp.concatenate(parts, axis=0)
            dkv = jnp.dot(both, qd2[...], preferred_element_type=F32)
            for u in range(GROUP):
                other = slots[g * GROUP + u]
                acc[other] = acc[other] + dkv[u * BLK:(u + 1) * BLK]
            keys = jnp.concatenate([kvt[slots[g * GROUP + u]] for u in range(GROUP)], axis=1)
            mixed = jnp.dot(keys, both, preferred_element_type=F32)
            return dq + mixed[0:HDIM, 0:BLK], at + mixed[HDIM:, BLK:]

        zero = jnp.zeros((HDIM, BLK), F32)
        dq, at = lax.fori_loop(0, steps, grads, (zero, zero))
        out_ref[i] = jnp.concatenate([dq * 0.125, at], axis=0).T.astype(BF)

    @pl.loop(0, HALF)
    def _(i):
        for e in range(2):
            dkv_ref[e, i] = acc[2 * i + e].astype(BF)


def greet_all(x, c, s):
    barrier = pltpu.get_barrier_semaphore()
    alone = c == s % 2
    dp = x * 2 + c

    def hello(device):
        pl.semaphore_signal(barrier, inc=1, device_id=device, device_id_type=MESH)

    @pl.loop(0, HALF)
    def _(j):
        @pl.when(jnp.logical_not(jnp.logical_and(alone, j == s // 2)))
        def _():
            hello(partner(x, c, s, j))

    @pl.loop(1, SCENES)
    def _(t):
        hello(((dp + t) % SCENES, s))

    @pl.loop(1, NB)
    def _(t):
        hello((dp, (s + t) % NB))

    owner = s // 4

    @pl.loop(0, SCENES)
    def _(t):
        k = 8 * (s % 4) + t

        @pl.when(jnp.logical_not(jnp.logical_and(owner == dp, k == s)))
        def _():
            hello((owner, k))

    keeps = 4 * dp + s // 8 == s
    total = HALF + SCENES - 1 + NB - 1 + SCENES
    pl.semaphore_wait(barrier, total - jnp.where(alone, 1, 0) - jnp.where(keeps, 1, 0))


def gather_kernel(
    od_ref, dkv_ref, w_ref, cot_ref,
    o_ref, dq_ref, dk_ref, dv_ref, wg_ref,
    ret_a, ret_b, sib, send_b, tiles, group, flat, send_w, recv_w, mine_w, stage,
    a_ss, a_rs, b_ss, b_rs, s_ss, s_rs, g_ss, g_rs, w_ss, w_rs, f_ss, f_rs,
):
    x, c, s = place()
    dp = x * 2 + c
    alone = c == s % 2
    mine = s // 2
    sibling = (x * 2 + 1 - c, s)
    greet_all(x, c, s)

    def is_self(j):
        return jnp.logical_and(alone, j == mine)

    def a_copy(j, slot):
        return pltpu.make_async_remote_copy(
            src_ref=od_ref.at[j], dst_ref=ret_a.at[slot], send_sem=a_ss.at[j], recv_sem=a_rs.at[slot],
            device_id=partner(x, c, s, j), device_id_type=MESH)

    def b_copy(j, slot):
        return pltpu.make_async_remote_copy(
            src_ref=send_b.at[j], dst_ref=ret_b.at[slot], send_sem=b_ss.at[j], recv_sem=b_rs.at[slot],
            device_id=partner(x, c, s, j), device_id_type=MESH)

    def s_copy(r):
        return pltpu.make_async_remote_copy(
            src_ref=dkv_ref.at[1 - c, pl.ds(r * 4, 4)], dst_ref=sib.at[pl.ds(r * 4, 4)],
            send_sem=s_ss.at[r], recv_sem=s_rs.at[r],
            device_id=sibling, device_id_type=MESH)

    def g_copy(p, slot):
        return pltpu.make_async_remote_copy(
            src_ref=tiles.at[p], dst_ref=group.at[slot], send_sem=g_ss.at[p], recv_sem=g_rs.at[slot],
            device_id=(p, s), device_id_type=MESH)

    def w_copy(k, slot):
        return pltpu.make_async_remote_copy(
            src_ref=send_w.at[k], dst_ref=recv_w.at[slot], send_sem=w_ss.at[k], recv_sem=w_rs.at[slot],
            device_id=(dp, k), device_id_type=MESH)

    def f_copy(p, slot):
        return pltpu.make_async_remote_copy(
            src_ref=mine_w, dst_ref=stage.at[slot], send_sem=f_ss.at[p], recv_sem=f_rs.at[slot],
            device_id=(p, 4 * dp + s // 8), device_id_type=MESH)

    @pl.loop(0, 4)
    def _(t):
        s_copy((t + s // 8) % 4).start()

    @pl.loop(0, HALF)
    def _(t):
        j = (t + mine) % HALF

        @pl.when(jnp.logical_not(is_self(j)))
        def _():
            a_copy(j, mine).start()

        @pl.when(is_self(j))
        def _():
            ret_a[mine] = od_ref[j]

    @pl.loop(0, 4)
    def _(t):
        r = (t + s // 8) % 4
        s_copy(r).wait_recv()

        @pl.loop(0, 4)
        def _(u):
            j = r * 4 + u
            send_b[j] = (dkv_ref[c, j].astype(F32) + sib[j].astype(F32)).astype(BF)

            @pl.when(jnp.logical_not(is_self(j)))
            def _():
                b_copy(j, mine).start()

            @pl.when(is_self(j))
            def _():
                ret_b[mine] = send_b[j]

    @pl.loop(0, HEADS // 2)
    def _(t):
        pair = (t + s // 4) % (HEADS // 2)
        cols = pl.ds(pl.multiple_of(pair * 128, 128), 128)
        for e in range(2):
            @pl.when(jnp.logical_not(is_self(pair * 2 + e)))
            def _():
                a_copy(pair * 2 + e, pair * 2 + e).wait_recv()

        a0 = ret_a[pair * 2]
        a1 = ret_a[pair * 2 + 1]
        at = jnp.concatenate([a0[:, 64:], a1[:, 64:]], axis=1)
        tiles[pair] = at

        @pl.when(pair != dp)
        def _():
            g_copy(pair, dp).start()

        @pl.when(pair == dp)
        def _():
            group[dp] = at

        dq_ref[:, cols] = jnp.concatenate([a0[:, 0:64], a1[:, 0:64]], axis=1)
        flat[:, cols] = at

    @pl.loop(0, SCENES)
    def _(p):
        @pl.when(p != dp)
        def _():
            g_copy(p, p).wait_recv()

    att = jnp.concatenate([group[p].T for p in range(SCENES)], axis=1)
    for q in range(4):
        part = jnp.dot(att, cot_ref[:, q * 256:(q + 1) * 256], preferred_element_type=F32).astype(BF)
        for r in range(8):
            send_w[r * 4 + q] = part[r * 16:(r + 1) * 16]

    @pl.loop(1, NB)
    def _(t):
        w_copy((s + t) % NB, s).start()

    recv_w[s] = send_w[s]

    @pl.loop(0, 4)
    def _(t):
        cols = pl.ds(pl.multiple_of(t * 256, 256), 256)
        o_ref[:, cols] = jnp.dot(flat[...], w_ref[:, cols], preferred_element_type=F32).astype(BF)

    @pl.loop(1, NB)
    def _(t):
        k = (s + NB - t) % NB
        w_copy(k, k).wait_recv()

    whole = recv_w[0].astype(F32)
    for k in range(1, NB):
        whole = whole + recv_w[k].astype(F32)
    mine_w[...] = whole * (SCENES * NB * BLK) ** (-0.5)
    keeps = 4 * dp + s // 8 == s

    @pl.loop(0, SCENES)
    def _(t):
        p = (dp + t) % SCENES
        local_end = jnp.logical_and(t == 0, keeps)

        @pl.when(jnp.logical_not(local_end))
        def _():
            f_copy(p, s % 8).start()

        @pl.when(local_end)
        def _():
            stage[s % 8] = mine_w[...]

    @pl.loop(0, HEADS // 2)
    def _(pair):
        cols = pl.ds(pl.multiple_of(pair * 128, 128), 128)
        for e in range(2):
            @pl.when(jnp.logical_not(is_self(pair * 2 + e)))
            def _():
                b_copy(pair * 2 + e, pair * 2 + e).wait_recv()

        a0 = ret_b[pair * 2]
        a1 = ret_b[pair * 2 + 1]
        dk_ref[:, cols] = jnp.concatenate([a0[:, 0:64], a1[:, 0:64]], axis=1)
        dv_ref[:, cols] = jnp.concatenate([a0[:, 64:], a1[:, 64:]], axis=1)

    @pl.loop(0, SCENES)
    def _(t):
        @pl.when(jnp.logical_not(jnp.logical_and(s // 4 == dp, 8 * (s % 4) + t == s)))
        def _():
            f_copy(dp, t).wait_recv()

    for t in range(SCENES):
        wg_ref[16 * (t // 4):16 * (t // 4) + 16, 256 * (t % 4):256 * (t % 4) + 256] = stage[t]

    @pl.loop(0, HALF)
    def _(j):
        @pl.when(jnp.logical_not(is_self(j)))
        def _():
            a_copy(j, mine).wait_send()
            b_copy(j, mine).wait_send()

    @pl.loop(0, 4)
    def _(r):
        s_copy(r).wait_send()

    @pl.loop(0, SCENES)
    def _(t):
        p = (dp + t) % SCENES

        @pl.when(t != 0)
        def _():
            g_copy(p, dp).wait_send()

        @pl.when(jnp.logical_not(jnp.logical_and(t == 0, keeps)))
        def _():
            f_copy(p, s % 8).wait_send()

    @pl.loop(1, NB)
    def _(t):
        w_copy((s + t) % NB, s).wait_send()


def spec(n):
    return [pl.BlockSpec(memory_space=VMEM)] * n


def attend(tab, kv, qd, parity):
    tile = lambda n, t: jax.ShapeDtypeStruct((n, BLK, BLK), t)
    return pl.pallas_call(
        core_kernel,
        out_shape=(tile(HALF, BF), jax.ShapeDtypeStruct((2, HALF, BLK, BLK), BF)),
        in_specs=[pl.BlockSpec(memory_space=pltpu.SMEM)] + spec(2) + [pl.BlockSpec(memory_space=pltpu.SMEM)],
        out_specs=tuple(spec(2)),
        scratch_shapes=[
            VMEM((NB, BLK, BLK), BF), VMEM((NB, BLK, BLK), F32),
            VMEM((SLOTS, BLK, BLK), F32), VMEM((SLOTS, BLK, BLK), F32),
            VMEM((2 * BLK, BLK), BF), VMEM((BLK, 2 * BLK), BF),
            pltpu.SMEM((SLOTS,), jnp.int32),
        ],
        compiler_params=pltpu.CompilerParams(vmem_limit_bytes=32 * 2**20),
        name="attend",
    )(tab, kv, qd, parity)


def local(node_queries, node_keys, node_values, cotangent, w_out, neighbours, contacts, ownership):
    cot_all = lax.all_gather(cotangent[0], "dp", axis=0, tiled=True)
    tile = lambda n, t: jax.ShapeDtypeStruct((n, BLK, BLK), t)
    flat = jax.ShapeDtypeStruct((BLK, HEADS * HDIM), BF)
    dma = pltpu.SemaphoreType.DMA
    table = jnp.concatenate([neighbours[0], contacts[0], ownership[0][:, None]], axis=1)
    table = jnp.pad(table, ((0, 0), (0, 128 - 13)))
    kv, qd, tab = pl.pallas_call(
        scatter_kernel,
        out_shape=(tile(NB, BF), tile(HALF, BF), jax.ShapeDtypeStruct((NB, 128), jnp.int32)),
        in_specs=spec(6),
        out_specs=tuple(spec(3)),
        scratch_shapes=[
            VMEM((HALF, BLK, BLK), BF), VMEM((HALF, BLK, BLK), BF), VMEM((NB, 128), jnp.int32),
            dma((HALF,)), dma((HALF,)), dma((HALF,)), dma((HALF,)), dma((HALF,)), dma((HALF,)), dma, dma,
        ],
        compiler_params=pltpu.CompilerParams(
            collective_id=0, has_side_effects=True, vmem_limit_bytes=32 * 2**20),
        name="scatter_heads",
    )(node_queries[0], node_keys[0], node_values[0], cotangent[0], w_out, table)

    parity = (lax.axis_index("dp") % 2).astype(jnp.int32).reshape(1)
    od, dkv = attend(tab, kv, qd, parity)

    output, dq, dk, dv, weight_grad = pl.pallas_call(
        gather_kernel,
        out_shape=(flat,) * 4 + (jax.ShapeDtypeStruct((NB, HEADS * HDIM), F32),),
        in_specs=spec(4),
        out_specs=tuple(spec(5)),
        scratch_shapes=[
            VMEM((HALF, BLK, BLK), BF), VMEM((HALF, BLK, BLK), BF), VMEM((HALF, BLK, BLK), BF), VMEM((HALF, BLK, BLK), BF),
            VMEM((SCENES, BLK, BLK), BF), VMEM((SCENES, BLK, BLK), BF), VMEM((BLK, HEADS * HDIM), BF),
            VMEM((NB, 16, 256), BF), VMEM((NB, 16, 256), BF), VMEM((16, 256), F32), VMEM((SCENES, 16, 256), F32),
            dma((HALF,)), dma((HALF,)), dma((HALF,)), dma((HALF,)), dma((4,)), dma((4,)),
            dma((SCENES,)), dma((SCENES,)), dma((NB,)), dma((NB,)), dma((SCENES,)), dma((SCENES,)),
        ],
        compiler_params=pltpu.CompilerParams(
            collective_id=1, has_side_effects=True, vmem_limit_bytes=32 * 2**20),
        name="gather_nodes",
    )(od, dkv, w_out, cot_all)
    return (output[None], dq[None], dk[None], dv[None], weight_grad)


def solution(mesh):
    placed = (
        P("dp", "seq", None), P("dp", "seq", None), P("dp", "seq", None), P("dp", "seq", None),
        P(), P("dp", None, None), P("dp", None, None), P("dp", None),
    )
    return jax.shard_map(
        local,
        mesh=mesh,
        in_specs=placed,
        out_specs=(
            P("dp", "seq", None), P("dp", "seq", None), P("dp", "seq", None), P("dp", "seq", None),
            P("seq", None),
        ),
        check_vma=False,
    )
```

```python
import functools

import jax
import jax.numpy as jnp
from jax import lax
from jax.experimental import pallas as pl
from jax.experimental.pallas import tpu as pltpu
from jax.sharding import PartitionSpec as P

HEADS = 16
HDIM = 64
BLK = 128
NB = 32
SCENES = 8
HALF = 16
SLOTS = 13
TILES = HALF * SLOTS
DIM = HEADS * HDIM
MESH = pl.DeviceIdType.MESH
VMEM = pltpu.VMEM
BF = jnp.bfloat16
F32 = jnp.float32


def place():
    dp = lax.axis_index("dp")
    s = lax.axis_index("seq")
    return dp // 2, dp % 2, s


def partner(x, c, s, j):
    return (x * 2 + s % 2, 2 * j + c)


def greet_all(x, c, s):
    barrier = pltpu.get_barrier_semaphore()
    alone = c == s % 2
    dp = x * 2 + c

    def hello(device):
        pl.semaphore_signal(barrier, inc=1, device_id=device, device_id_type=MESH)

    @pl.loop(0, HALF)
    def _(j):
        @pl.when(jnp.logical_not(jnp.logical_and(alone, j == s // 2)))
        def _():
            hello(partner(x, c, s, j))

    @pl.loop(1, SCENES)
    def _(t):
        hello(((dp + t) % SCENES, s))

    y, z = s // 8, s % 8

    @pl.loop(1, 4)
    def _(t):
        hello((dp, (y + t) % 4 * 8 + z))

    @pl.loop(1, 8)
    def _(t):
        hello((dp, y * 8 + (z + t) % 8))

    owner = s // 4

    @pl.loop(0, SCENES)
    def _(t):
        k = 8 * (s % 4) + t

        @pl.when(jnp.logical_not(jnp.logical_and(owner == dp, k == s)))
        def _():
            hello((owner, k))

    keeps = 4 * dp + s // 8 == s
    total = HALF + SCENES - 1 + 3 + 7 + SCENES
    pl.semaphore_wait(barrier, total - jnp.where(alone, 1, 0) - jnp.where(keeps, 1, 0))


def fused_kernel(
    q_hbm, k_hbm, v_hbm, cot_hbm, w_hbm, near_ref, touch_ref, own_ref,
    o_ref, dq_ref, dk_ref, dv_ref, wg_ref,
    q_ref, k_ref, v_ref, w_ref, cot_ref,
    send_kv, send_qd, kv_ref, kvt_ref, qd_ref,
    lists, lists_sib, table, table_s,
    sbuf, pbuf, qd2, qd2t, parts, od_ref, sib_out,
    ret_a, ret_b, sib, send_b, tiles, group, flat, send_y, recv_y, send_z, recv_z, mine_w, stage,
    in_s, kv_ss, kv_rs, qd_ss, qd_rs, re_ss, re_rs, tb_ss, tb_rs, ts_s, cx_ss, cx_rs, cc_ss, cc_rs,
    a_ss, a_rs, b_ss, b_rs, s_ss, s_rs, g_ss, g_rs, y_ss, y_rs, z_ss, z_rs, f_ss, f_rs,
):
    x, c, s = place()
    dp = x * 2 + c
    y, z = s // 8, s % 8
    alone = c == s % 2
    mine = s // 2
    sibling = (x * 2 + 1 - c, s)

    loads = [
        pltpu.make_async_copy(src, dst, in_s.at[n])
        for n, (src, dst) in enumerate(
            ((k_hbm, k_ref), (v_hbm, v_ref), (cot_hbm, cot_ref.at[dp]), (w_hbm, w_ref), (q_hbm, q_ref)))
    ]
    for load in loads:
        load.start()

    def is_self(j):
        return jnp.logical_and(alone, j == mine)

    def remote(src, dst, send, recv, device):
        return pltpu.make_async_remote_copy(
            src_ref=src, dst_ref=dst, send_sem=send, recv_sem=recv, device_id=device, device_id_type=MESH)

    def kv_copy(j, block, slot):
        return remote(send_kv.at[j], kv_ref.at[block], kv_ss.at[j], kv_rs.at[slot], partner(x, c, s, j))

    def qd_copy(j, slot):
        return remote(send_qd.at[j], qd_ref.at[slot], qd_ss.at[j], qd_rs.at[slot], partner(x, c, s, j))

    def relay(j, odd):
        return remote(kv_ref.at[2 * j + odd], kv_ref.at[2 * j + odd], re_ss.at[j], re_rs.at[j], sibling)

    def cot_across(other, source):
        return remote(cot_ref.at[source * 2 + c], cot_ref.at[source * 2 + c], cx_ss.at[other], cx_rs.at[source],
                      (other * 2 + c, s))

    def cot_beside(source, core):
        return remote(cot_ref.at[source * 2 + core], cot_ref.at[source * 2 + core], cc_ss.at[source], cc_rs.at[source],
                      sibling)

    def a_copy(j, slot):
        return remote(od_ref.at[j], ret_a.at[slot], a_ss.at[j], a_rs.at[slot], partner(x, c, s, j))

    def b_copy(j, slot):
        return remote(send_b.at[j], ret_b.at[slot], b_ss.at[j], b_rs.at[slot], partner(x, c, s, j))

    def s_copy(r):
        return remote(sib_out.at[pl.ds(r * 4, 4)], sib.at[pl.ds(r * 4, 4)], s_ss.at[r], s_rs.at[r], sibling)

    def g_copy(p, slot):
        return remote(tiles.at[p], group.at[slot], g_ss.at[p], g_rs.at[slot], (p, s))

    def y_copy(k, slot):
        return remote(send_y.at[pl.ds(k * 8, 8)], recv_y.at[slot], y_ss.at[k], y_rs.at[slot], (dp, k * 8 + z))

    def z_copy(k, slot):
        return remote(send_z.at[k], recv_z.at[slot], z_ss.at[k], z_rs.at[slot], (dp, y * 8 + k))

    def f_copy(p, slot):
        return remote(mine_w, stage.at[slot], f_ss.at[p], f_rs.at[slot], (p, 4 * dp + s // 8))

    lists[...] = jnp.full((BLK, BLK), -1, jnp.int32)
    lists[0:NB, 0:4] = near_ref[...]
    lists[0:NB, 4:12] = touch_ref[...]
    lists[NB:NB + 1, 0:NB] = own_ref[...]
    loads[0].wait()
    loads[1].wait()
    greet_all(x, c, s)
    list_copy = remote(lists, lists_sib, tb_ss, tb_rs, sibling)
    list_copy.start()

    @pl.loop(0, HEADS // 2)
    def _(t):
        pair = (t + s // 4) % (HEADS // 2)
        cols = pl.ds(pl.multiple_of(pair * 128, 128), 128)
        k = k_ref[:, cols]
        v = v_ref[:, cols]
        for e in range(2):
            j = pair * 2 + e
            send_kv[j] = jnp.concatenate([k[:, e * 64:e * 64 + 64], v[:, e * 64:e * 64 + 64]], axis=1)

            @pl.when(jnp.logical_not(is_self(j)))
            def _():
                kv_copy(j, s, mine).start()

            @pl.when(is_self(j))
            def _():
                kv_ref[s] = send_kv[j]

    for load in loads[2:]:
        load.wait()

    @pl.loop(0, HEADS // 2)
    def _(t):
        pair = (t + s // 4) % (HEADS // 2)
        cols = pl.ds(pl.multiple_of(pair * 128, 128), 128)
        q = q_ref[:, cols] * jnp.asarray(0.125, BF)
        d = lax.dot_general(cot_ref[dp], w_ref[cols, :], (((1,), (1,)), ((), ())),
                            preferred_element_type=F32).astype(BF)
        for e in range(2):
            j = pair * 2 + e
            send_qd[j] = jnp.concatenate([q[:, e * 64:e * 64 + 64], d[:, e * 64:e * 64 + 64]], axis=1)

            @pl.when(jnp.logical_not(is_self(j)))
            def _():
                qd_copy(j, mine).start()

            @pl.when(is_self(j))
            def _():
                qd_ref[mine] = send_qd[j]

    cot_beside(x, c).start()

    @pl.loop(1, 4)
    def _(t):
        cot_across((x + t) % 4, x).start()

    list_copy.wait()
    own = jnp.broadcast_to(alone.astype(jnp.int32), (BLK, BLK))
    chosen = lists[...] * own + lists_sib[...] * (1 - own)
    turned = chosen.T
    key_id = lax.broadcasted_iota(jnp.int32, (NB, BLK), 0)
    block_id = lax.broadcasted_iota(jnp.int32, (NB, BLK), 1)
    lane = lax.broadcasted_iota(jnp.int32, (1, BLK), 1)
    first = block_id // 2 * SLOTS
    owner_row = jnp.broadcast_to(chosen[NB:NB + 1, :], (NB, BLK))
    owner_col = jnp.broadcast_to(turned[0:NB, NB:NB + 1], (NB, BLK))
    pos = jnp.where(key_id == block_id, first, TILES)
    table[NB:NB + 1, :] = lane
    table[NB + 16:NB + 17, :] = jnp.ones((1, BLK), jnp.int32)
    for e in range(12):
        entry = turned[e:e + 1, :]
        match = jnp.broadcast_to(entry, (NB, BLK)) == key_id
        if e >= 4:
            match = jnp.logical_and(match, owner_row != owner_col)
        valid = jnp.max(jnp.where(match, 1, 0), axis=0, keepdims=True)
        pos = jnp.where(match, first + (e + 1), pos)
        table[NB + 1 + e:NB + 2 + e, :] = jnp.where(valid > 0, entry, lane)
        table[NB + 17 + e:NB + 18 + e, :] = valid
    table[0:NB, :] = pos
    to_scalar = pltpu.make_async_copy(table, table_s, ts_s)
    to_scalar.start()
    to_scalar.wait()

    qd2[...] = jnp.zeros((2 * BLK, BLK), BF)
    qd2t[...] = jnp.zeros((BLK, 2 * BLK), BF)
    parts[TILES] = jnp.zeros((BLK, BLK), BF)

    @pl.loop(0, HALF)
    def _(t):
        j = (t + mine) % HALF

        @pl.when(jnp.logical_not(is_self(j)))
        def _():
            kv_copy(j, 2 * j + c, j).wait_recv()

        relay(j, c).start()
        kvt_ref[2 * j + c] = kv_ref[2 * j + c].T

    @pl.loop(0, HALF)
    def _(t):
        j = (t + mine) % HALF
        relay(j, 1 - c).wait_recv()
        kvt_ref[2 * j + 1 - c] = kv_ref[2 * j + 1 - c].T

    def fold(part):
        return part.reshape(BLK // 8, 8, BLK)

    spans = [(e, min(2, SLOTS - e)) for e in range(0, SLOTS, 2)]

    @pl.loop(0, HALF)
    def _(t):
        i = 2 * ((mine // 2 - t // 2 + 8) % 8) + t % 2
        b = 2 * i + c

        @pl.when(jnp.logical_not(is_self(i)))
        def _():
            qd_copy(i, i).wait_recv()

        @pl.when(t == 6)
        def _():
            @pl.loop(1, 4)
            def _(u):
                cot_across(x, (x + u) % 4).wait_recv()
                cot_beside((x + u) % 4, c).start()

        slots = [jnp.clip(table_s[NB + e, b], 0, NB - 1) for e in range(SLOTS)]
        qd = qd_ref[i]
        qdt = qd.T
        qd2[0:BLK, 0:HDIM] = qd[:, 0:HDIM]
        qd2[BLK:, HDIM:] = qd[:, HDIM:]
        qd2t[0:HDIM, 0:BLK] = qdt[0:HDIM, :]
        qd2t[HDIM:, BLK:] = qdt[HDIM:, :]

        m = None
        for e, width in spans:
            keys = jnp.concatenate([kv_ref[slots[e + u]] for u in range(width)], axis=0)
            both = jnp.dot(keys, qd2t[...], preferred_element_type=F32)
            for u in range(width):
                part = both[u * BLK:(u + 1) * BLK, 0:BLK]
                if e + u > 0:
                    part = part + (table_s[NB + 16 + e + u, b] - 1).astype(F32) * 1e30
                sbuf[e + u] = part
                pbuf[e + u] = both[u * BLK:(u + 1) * BLK, BLK:]
                top = jnp.max(fold(part), axis=0)
                m = top if m is None else jnp.maximum(m, top)
        m = jnp.broadcast_to(jnp.max(m, axis=0, keepdims=True), (8, BLK))
        total = jnp.zeros((8, BLK), F32)
        dot = jnp.zeros((8, BLK), F32)
        for e in range(SLOTS):
            part = jnp.exp(fold(sbuf[e]) - m[None])
            sbuf[e] = part.reshape(BLK, BLK)
            total = total + jnp.sum(part, axis=0)
            dot = dot + jnp.sum(part * fold(pbuf[e]), axis=0)
        inv = 1.0 / jnp.sum(total, axis=0, keepdims=True)
        delta = jnp.broadcast_to(jnp.sum(dot, axis=0, keepdims=True) * inv, (8, BLK))
        inv = jnp.broadcast_to(inv, (8, BLK))
        mixed = None
        for e, width in spans:
            pieces = []
            for u in range(width):
                prob = fold(sbuf[e + u]) * inv[None]
                ds = prob * (fold(pbuf[e + u]) - delta[None])
                pieces.append(jnp.concatenate(
                    [ds.reshape(BLK, BLK).astype(BF), prob.reshape(BLK, BLK).astype(BF)], axis=1))
            both = jnp.concatenate(pieces, axis=0)
            dkv = jnp.dot(both, qd2[...], preferred_element_type=F32)
            for u in range(width):
                parts[i * SLOTS + e + u] = dkv[u * BLK:(u + 1) * BLK].astype(BF)
            keys = jnp.concatenate([kvt_ref[slots[e + u]] for u in range(width)], axis=1)
            term = jnp.dot(keys, both, preferred_element_type=F32)
            term = (term[0:HDIM, 0:BLK], term[HDIM:, BLK:])
            mixed = term if mixed is None else (mixed[0] + term[0], mixed[1] + term[1])
        od_ref[i] = jnp.concatenate([mixed[0] * 0.125, mixed[1]], axis=0).T.astype(BF)

        @pl.when(jnp.logical_not(is_self(i)))
        def _():
            a_copy(i, mine).start()

        @pl.when(is_self(i))
        def _():
            ret_a[mine] = od_ref[i]

    def gathered(key):
        whole = None
        for i in range(HALF):
            part = parts[jnp.clip(table_s[key, 2 * i + c], 0, TILES)].astype(F32)
            whole = part if whole is None else whole + part
        return whole

    @pl.loop(0, 4)
    def _(t):
        r = (t + s // 8) % 4

        @pl.loop(0, 4)
        def _(u):
            j = r * 4 + u
            sib_out[j] = gathered(2 * j + 1 - c).astype(BF)

        s_copy(r).start()

    def back_chunk(t):
        r = (t + s // 8) % 4
        s_copy(r).wait_recv()

        @pl.loop(0, 4)
        def _(u):
            j = r * 4 + u
            send_b[j] = (gathered(2 * j + c) + sib[j].astype(F32)).astype(BF)

            @pl.when(jnp.logical_not(is_self(j)))
            def _():
                b_copy(j, mine).start()

            @pl.when(is_self(j))
            def _():
                ret_b[mine] = send_b[j]

    @pl.loop(0, HEADS // 2)
    def _(t):
        pair = (t + s // 4) % (HEADS // 2)
        cols = pl.ds(pl.multiple_of(pair * 128, 128), 128)
        for e in range(2):
            @pl.when(jnp.logical_not(is_self(pair * 2 + e)))
            def _():
                a_copy(pair * 2 + e, pair * 2 + e).wait_recv()

        a0 = ret_a[pair * 2]
        a1 = ret_a[pair * 2 + 1]
        at = jnp.concatenate([a0[:, 64:], a1[:, 64:]], axis=1)
        tiles[pair] = at

        @pl.when(pair != dp)
        def _():
            g_copy(pair, dp).start()

        @pl.when(pair == dp)
        def _():
            group[dp] = at

        dq_ref[:, cols] = jnp.concatenate([a0[:, 0:64], a1[:, 0:64]], axis=1)
        flat[:, cols] = at

    @pl.loop(0, 2)
    def _(t):
        back_chunk(t)

    cot_beside(x, 1 - c).wait_recv()

    @pl.loop(1, 4)
    def _(u):
        cot_beside((x + u) % 4, 1 - c).wait_recv()

    @pl.loop(0, SCENES)
    def _(p):
        @pl.when(p != dp)
        def _():
            g_copy(p, p).wait_recv()

    att = jnp.concatenate([group[p].T for p in range(SCENES)], axis=1)
    for q in range(4):
        grads = jnp.concatenate([cot_ref[p, :, q * 256:(q + 1) * 256] for p in range(SCENES)], axis=0)
        part = jnp.dot(att, grads, preferred_element_type=F32).astype(BF)
        for r in range(8):
            send_y[r * 4 + q] = part[r * 16:(r + 1) * 16]

    @pl.loop(1, 4)
    def _(t):
        y_copy((y + t) % 4, y).start()

    recv_y[y] = send_y[pl.ds(y * 8, 8)]

    @pl.loop(2, 4)
    def _(t):
        back_chunk(t)

    @pl.loop(1, 4)
    def _(t):
        k = (y + 4 - t) % 4
        y_copy(k, k).wait_recv()

    for k in range(8):
        send_z[k] = (recv_y[0, k].astype(F32) + recv_y[1, k].astype(F32) + recv_y[2, k].astype(F32)
                     + recv_y[3, k].astype(F32)).astype(BF)

    @pl.loop(1, 8)
    def _(t):
        z_copy((z + t) % 8, z).start()

    recv_z[z] = send_z[z]

    @pl.loop(0, 4)
    def _(t):
        cols = pl.ds(pl.multiple_of(t * 256, 256), 256)
        o_ref[:, cols] = jnp.dot(flat[...], w_ref[:, cols], preferred_element_type=F32).astype(BF)

    @pl.loop(1, 8)
    def _(t):
        k = (z + 8 - t) % 8
        z_copy(k, k).wait_recv()

    whole = recv_z[0].astype(F32)
    for k in range(1, 8):
        whole = whole + recv_z[k].astype(F32)
    mine_w[...] = whole * (SCENES * NB * BLK) ** (-0.5)
    keeps = 4 * dp + s // 8 == s

    @pl.loop(0, SCENES)
    def _(t):
        p = (dp + t) % SCENES
        local_end = jnp.logical_and(t == 0, keeps)

        @pl.when(jnp.logical_not(local_end))
        def _():
            f_copy(p, s % 8).start()

        @pl.when(local_end)
        def _():
            stage[s % 8] = mine_w[...]

    @pl.loop(0, HEADS // 2)
    def _(pair):
        cols = pl.ds(pl.multiple_of(pair * 128, 128), 128)
        for e in range(2):
            @pl.when(jnp.logical_not(is_self(pair * 2 + e)))
            def _():
                b_copy(pair * 2 + e, pair * 2 + e).wait_recv()

        a0 = ret_b[pair * 2]
        a1 = ret_b[pair * 2 + 1]
        dk_ref[:, cols] = jnp.concatenate([a0[:, 0:64], a1[:, 0:64]], axis=1)
        dv_ref[:, cols] = jnp.concatenate([a0[:, 64:], a1[:, 64:]], axis=1)

    @pl.loop(0, SCENES)
    def _(t):
        @pl.when(jnp.logical_not(jnp.logical_and(s // 4 == dp, 8 * (s % 4) + t == s)))
        def _():
            f_copy(dp, t).wait_recv()

    for t in range(SCENES):
        wg_ref[16 * (t // 4):16 * (t // 4) + 16, 256 * (t % 4):256 * (t % 4) + 256] = stage[t]

    @pl.loop(0, HALF)
    def _(j):
        relay(j, c).wait_send()

        @pl.when(jnp.logical_not(is_self(j)))
        def _():
            kv_copy(j, s, mine).wait_send()
            qd_copy(j, mine).wait_send()
            a_copy(j, mine).wait_send()
            b_copy(j, mine).wait_send()

    @pl.loop(0, 4)
    def _(r):
        s_copy(r).wait_send()
        cot_beside(r, c).wait_send()

        @pl.when(r != x)
        def _():
            cot_across(r, x).wait_send()

    @pl.loop(0, SCENES)
    def _(t):
        p = (dp + t) % SCENES

        @pl.when(t != 0)
        def _():
            g_copy(p, dp).wait_send()

        @pl.when(jnp.logical_not(jnp.logical_and(t == 0, keeps)))
        def _():
            f_copy(p, s % 8).wait_send()

    @pl.loop(1, 4)
    def _(t):
        y_copy((y + t) % 4, y).wait_send()

    @pl.loop(1, 8)
    def _(t):
        z_copy((z + t) % 8, z).wait_send()


def local(node_queries, node_keys, node_values, cotangent, w_out, neighbours, contacts, ownership):
    flat = jax.ShapeDtypeStruct((BLK, DIM), BF)
    dma = pltpu.SemaphoreType.DMA
    rows = VMEM((BLK, DIM), BF)
    wide = lambda n, t=BF: VMEM((n, BLK, BLK), t)
    vmem = pl.BlockSpec(memory_space=VMEM)
    output, dq, dk, dv, weight_grad = pl.pallas_call(
        fused_kernel,
        out_shape=(flat,) * 4 + (jax.ShapeDtypeStruct((NB, DIM), F32),),
        in_specs=[pl.BlockSpec(memory_space=pltpu.HBM)] * 5 + [vmem] * 3,
        out_specs=(vmem,) * 5,
        scratch_shapes=[
            rows, rows, rows, VMEM((DIM, DIM), BF), VMEM((SCENES, BLK, DIM), BF),
            wide(HALF), wide(HALF), wide(NB), wide(NB), wide(HALF),
            VMEM((BLK, BLK), jnp.int32), VMEM((BLK, BLK), jnp.int32), VMEM((64, BLK), jnp.int32), pltpu.SMEM((64, BLK), jnp.int32),
            wide(SLOTS, F32), wide(SLOTS, F32), VMEM((2 * BLK, BLK), BF), VMEM((BLK, 2 * BLK), BF),
            wide(TILES + 1), wide(HALF), wide(HALF),
            wide(HALF), wide(HALF), wide(HALF), wide(HALF), wide(SCENES), wide(SCENES), rows,
            VMEM((NB, 16, 256), BF), VMEM((4, 8, 16, 256), BF), VMEM((8, 16, 256), BF), VMEM((8, 16, 256), BF),
            VMEM((16, 256), F32), VMEM((SCENES, 16, 256), F32),
            dma((5,)), dma((HALF,)), dma((HALF,)), dma((HALF,)), dma((HALF,)), dma((HALF,)), dma((HALF,)), dma, dma, dma,
            dma((4,)), dma((4,)), dma((4,)), dma((4,)),
            dma((HALF,)), dma((HALF,)), dma((HALF,)), dma((HALF,)), dma((4,)), dma((4,)),
            dma((SCENES,)), dma((SCENES,)), dma((4,)), dma((4,)), dma((8,)), dma((8,)), dma((SCENES,)), dma((SCENES,)),
        ],
        compiler_params=pltpu.CompilerParams(
            collective_id=0, has_side_effects=True, vmem_limit_bytes=48 * 2**20),
        name="sublayer",
    )(node_queries[0], node_keys[0], node_values[0], cotangent[0], w_out, neighbours[0], contacts[0], ownership)
    return (output[None], dq[None], dk[None], dv[None], weight_grad)


def solution(mesh):
    placed = (
        P("dp", "seq", None), P("dp", "seq", None), P("dp", "seq", None), P("dp", "seq", None),
        P(), P("dp", None, None), P("dp", None, None), P("dp", None),
    )
    return jax.shard_map(
        local,
        mesh=mesh,
        in_specs=placed,
        out_specs=(
            P("dp", "seq", None), P("dp", "seq", None), P("dp", "seq", None), P("dp", "seq", None),
            P("seq", None),
        ),
        check_vma=False,
    )
```

```python
import functools

import jax
import jax.numpy as jnp
from jax import lax
from jax.experimental import pallas as pl
from jax.experimental.pallas import tpu as pltpu
from jax.sharding import PartitionSpec as P

HEADS = 16
HDIM = 64
BLK = 128
NB = 32
SCENES = 8
HALF = 16
SLOTS = 13
TILES = HALF * SLOTS
DIM = HEADS * HDIM
MESH = pl.DeviceIdType.MESH
VMEM = pltpu.VMEM
BF = jnp.bfloat16
F32 = jnp.float32


def place():
    dp = lax.axis_index("dp")
    s = lax.axis_index("seq")
    return dp // 2, dp % 2, s


def partner(x, c, s, j):
    return (x * 2 + s % 2, 2 * j + c)


def greet_all(x, c, s):
    barrier = pltpu.get_barrier_semaphore()
    alone = c == s % 2
    dp = x * 2 + c

    def hello(device):
        pl.semaphore_signal(barrier, inc=1, device_id=device, device_id_type=MESH)

    @pl.loop(0, HALF)
    def _(j):
        @pl.when(jnp.logical_not(jnp.logical_and(alone, j == s // 2)))
        def _():
            hello(partner(x, c, s, j))

    @pl.loop(1, SCENES)
    def _(t):
        hello(((dp + t) % SCENES, s))

    y, z = s // 8, s % 8

    @pl.loop(1, 4)
    def _(t):
        hello((dp, (y + t) % 4 * 8 + z))

    @pl.loop(1, 8)
    def _(t):
        hello((dp, y * 8 + (z + t) % 8))

    owner = s // 4

    @pl.loop(0, SCENES)
    def _(t):
        k = 8 * (s % 4) + t

        @pl.when(jnp.logical_not(jnp.logical_and(owner == dp, k == s)))
        def _():
            hello((owner, k))

    keeps = 4 * dp + s // 8 == s
    total = HALF + SCENES - 1 + 3 + 7 + SCENES
    pl.semaphore_wait(barrier, total - jnp.where(alone, 1, 0) - jnp.where(keeps, 1, 0))


def fused_kernel(
    q_hbm, k_hbm, v_hbm, cot_hbm, w_hbm, near_ref, touch_ref, own_ref,
    o_ref, dq_ref, dk_ref, dv_ref, wg_ref,
    q_ref, k_ref, v_ref, w_ref, cot_ref,
    send_kv, send_qd, kv_ref, kvt_ref, qd_ref,
    lists, lists_sib, table, table_s,
    sbuf, pbuf, qd2, qd2t, parts, od_ref, sib_out,
    ret_a, ret_b, sib, send_b, tiles, group, flat, send_y, recv_y, send_z, recv_z, mine_w, stage,
    in_s, kv_ss, kv_rs, qd_ss, qd_rs, re_ss, re_rs, tb_ss, tb_rs, ts_s, cx_ss, cx_rs, cc_ss, cc_rs,
    a_ss, a_rs, b_ss, b_rs, s_ss, s_rs, g_ss, g_rs, y_ss, y_rs, z_ss, z_rs, f_ss, f_rs,
):
    x, c, s = place()
    dp = x * 2 + c
    y, z = s // 8, s % 8
    alone = c == s % 2
    mine = s // 2
    sibling = (x * 2 + 1 - c, s)

    loads = [
        pltpu.make_async_copy(src, dst, in_s.at[n])
        for n, (src, dst) in enumerate(
            ((k_hbm, k_ref), (v_hbm, v_ref), (cot_hbm, cot_ref.at[dp]), (w_hbm, w_ref), (q_hbm, q_ref)))
    ]
    for load in loads:
        load.start()

    def is_self(j):
        return jnp.logical_and(alone, j == mine)

    def remote(src, dst, send, recv, device):
        return pltpu.make_async_remote_copy(
            src_ref=src, dst_ref=dst, send_sem=send, recv_sem=recv, device_id=device, device_id_type=MESH)

    def kv_copy(j, block, slot):
        return remote(send_kv.at[j], kv_ref.at[block], kv_ss.at[j], kv_rs.at[slot], partner(x, c, s, j))

    def qd_copy(j, slot):
        return remote(send_qd.at[j], qd_ref.at[slot], qd_ss.at[j], qd_rs.at[slot], partner(x, c, s, j))

    def relay(j, odd):
        return remote(kv_ref.at[2 * j + odd], kv_ref.at[2 * j + odd], re_ss.at[j], re_rs.at[j], sibling)

    def cot_across(other, source):
        return remote(cot_ref.at[source * 2 + c], cot_ref.at[source * 2 + c], cx_ss.at[other], cx_rs.at[source],
                      (other * 2 + c, s))

    def cot_beside(source, core):
        return remote(cot_ref.at[source * 2 + core], cot_ref.at[source * 2 + core], cc_ss.at[source], cc_rs.at[source],
                      sibling)

    def a_copy(j, slot):
        return remote(od_ref.at[j], ret_a.at[slot], a_ss.at[j], a_rs.at[slot], partner(x, c, s, j))

    def b_copy(j, slot):
        return remote(send_b.at[j], ret_b.at[slot], b_ss.at[j], b_rs.at[slot], partner(x, c, s, j))

    def s_copy(r):
        return remote(sib_out.at[pl.ds(r * 4, 4)], sib.at[pl.ds(r * 4, 4)], s_ss.at[r], s_rs.at[r], sibling)

    def g_copy(p, slot):
        return remote(tiles.at[p], group.at[slot], g_ss.at[p], g_rs.at[slot], (p, s))

    def y_copy(k, slot):
        return remote(send_y.at[pl.ds(k * 8, 8)], recv_y.at[slot], y_ss.at[k], y_rs.at[slot], (dp, k * 8 + z))

    def z_copy(k, slot):
        return remote(send_z.at[k], recv_z.at[slot], z_ss.at[k], z_rs.at[slot], (dp, y * 8 + k))

    def f_copy(p, slot):
        return remote(mine_w, stage.at[slot], f_ss.at[p], f_rs.at[slot], (p, 4 * dp + s // 8))

    lists[...] = jnp.full((BLK, BLK), -1, jnp.int32)
    lists[0:NB, 0:4] = near_ref[...]
    lists[0:NB, 4:12] = touch_ref[...]
    lists[NB:NB + 1, 0:NB] = own_ref[...]
    loads[0].wait()
    loads[1].wait()
    greet_all(x, c, s)
    list_copy = remote(lists, lists_sib, tb_ss, tb_rs, sibling)
    list_copy.start()

    @pl.loop(0, HEADS // 2)
    def _(t):
        pair = (t + s // 4) % (HEADS // 2)
        cols = pl.ds(pl.multiple_of(pair * 128, 128), 128)
        k = k_ref[:, cols]
        v = v_ref[:, cols]
        for e in range(2):
            j = pair * 2 + e
            send_kv[j] = jnp.concatenate([k[:, e * 64:e * 64 + 64], v[:, e * 64:e * 64 + 64]], axis=1)

            @pl.when(jnp.logical_not(is_self(j)))
            def _():
                kv_copy(j, s, mine).start()

            @pl.when(is_self(j))
            def _():
                kv_ref[s] = send_kv[j]

    for load in loads[2:]:
        load.wait()

    @pl.loop(0, HEADS // 2)
    def _(t):
        pair = (t + s // 4) % (HEADS // 2)
        cols = pl.ds(pl.multiple_of(pair * 128, 128), 128)
        q = q_ref[:, cols] * jnp.asarray(0.125, BF)
        d = lax.dot_general(cot_ref[dp], w_ref[cols, :], (((1,), (1,)), ((), ())),
                            preferred_element_type=F32).astype(BF)
        for e in range(2):
            j = pair * 2 + e
            send_qd[j] = jnp.concatenate([q[:, e * 64:e * 64 + 64], d[:, e * 64:e * 64 + 64]], axis=1)

            @pl.when(jnp.logical_not(is_self(j)))
            def _():
                qd_copy(j, mine).start()

            @pl.when(is_self(j))
            def _():
                qd_ref[mine] = send_qd[j]

    cot_beside(x, c).start()

    @pl.loop(1, 4)
    def _(t):
        cot_across((x + t) % 4, x).start()

    list_copy.wait()
    own = jnp.broadcast_to(alone.astype(jnp.int32), (BLK, BLK))
    chosen = lists[...] * own + lists_sib[...] * (1 - own)
    turned = chosen.T
    key_id = lax.broadcasted_iota(jnp.int32, (NB, BLK), 0)
    block_id = lax.broadcasted_iota(jnp.int32, (NB, BLK), 1)
    lane = lax.broadcasted_iota(jnp.int32, (1, BLK), 1)
    first = block_id // 2 * SLOTS
    owner_row = jnp.broadcast_to(chosen[NB:NB + 1, :], (NB, BLK))
    owner_col = jnp.broadcast_to(turned[0:NB, NB:NB + 1], (NB, BLK))
    pos = jnp.where(key_id == block_id, first, TILES)
    table[NB:NB + 1, :] = lane
    table[NB + 16:NB + 17, :] = jnp.ones((1, BLK), jnp.int32)
    for e in range(12):
        entry = turned[e:e + 1, :]
        match = jnp.broadcast_to(entry, (NB, BLK)) == key_id
        if e >= 4:
            match = jnp.logical_and(match, owner_row != owner_col)
        valid = jnp.max(jnp.where(match, 1, 0), axis=0, keepdims=True)
        pos = jnp.where(match, first + (e + 1), pos)
        table[NB + 1 + e:NB + 2 + e, :] = jnp.where(valid > 0, entry, lane)
        table[NB + 17 + e:NB + 18 + e, :] = valid
    table[0:NB, :] = pos
    to_scalar = pltpu.make_async_copy(table, table_s, ts_s)
    to_scalar.start()
    to_scalar.wait()

    qd2[...] = jnp.zeros((2, 2 * BLK, BLK), BF)
    qd2t[...] = jnp.zeros((2, BLK, 2 * BLK), BF)
    parts[TILES] = jnp.zeros((BLK, BLK), BF)

    @pl.loop(0, HALF)
    def _(t):
        j = (t + mine) % HALF

        @pl.when(jnp.logical_not(is_self(j)))
        def _():
            kv_copy(j, 2 * j + c, j).wait_recv()

        relay(j, c).start()
        kvt_ref[2 * j + c] = kv_ref[2 * j + c].T

    @pl.loop(0, HALF)
    def _(t):
        j = (t + mine) % HALF
        relay(j, 1 - c).wait_recv()
        kvt_ref[2 * j + 1 - c] = kv_ref[2 * j + 1 - c].T

    def fold(part):
        return part.reshape(BLK // 8, 8, BLK)

    spans = [(e, min(2, SLOTS - e)) for e in range(0, SLOTS, 2)]

    def attend(i, k):
        b = 2 * i + c
        slots = [jnp.clip(table_s[NB + e, b], 0, NB - 1) for e in range(SLOTS)]
        qd = qd_ref[i]
        qdt = qd.T
        qd2[k, 0:BLK, 0:HDIM] = qd[:, 0:HDIM]
        qd2[k, BLK:, HDIM:] = qd[:, HDIM:]
        qd2t[k, 0:HDIM, 0:BLK] = qdt[0:HDIM, :]
        qd2t[k, HDIM:, BLK:] = qdt[HDIM:, :]
        yield True
        m = None
        for e, width in spans:
            keys = jnp.concatenate([kv_ref[slots[e + u]] for u in range(width)], axis=0)
            both = jnp.dot(keys, qd2t[k], preferred_element_type=F32)
            for u in range(width):
                part = both[u * BLK:(u + 1) * BLK, 0:BLK]
                if e + u > 0:
                    part = part + (table_s[NB + 16 + e + u, b] - 1).astype(F32) * 1e30
                sbuf[k * SLOTS + e + u] = part
                pbuf[k * SLOTS + e + u] = both[u * BLK:(u + 1) * BLK, BLK:]
                top = jnp.max(fold(part), axis=0)
                m = top if m is None else jnp.maximum(m, top)
        m = jnp.broadcast_to(jnp.max(m, axis=0, keepdims=True), (8, BLK))
        yield True
        total = jnp.zeros((8, BLK), F32)
        dot = jnp.zeros((8, BLK), F32)
        for e in range(SLOTS):
            part = jnp.exp(fold(sbuf[k * SLOTS + e]) - m[None])
            sbuf[k * SLOTS + e] = part.reshape(BLK, BLK)
            total = total + jnp.sum(part, axis=0)
            dot = dot + jnp.sum(part * fold(pbuf[k * SLOTS + e]), axis=0)
        yield True
        inv = 1.0 / jnp.sum(total, axis=0, keepdims=True)
        delta = jnp.broadcast_to(jnp.sum(dot, axis=0, keepdims=True) * inv, (8, BLK))
        inv = jnp.broadcast_to(inv, (8, BLK))
        mixed = None
        for e, width in spans:
            pieces = []
            for u in range(width):
                prob = fold(sbuf[k * SLOTS + e + u]) * inv[None]
                ds = prob * (fold(pbuf[k * SLOTS + e + u]) - delta[None])
                pieces.append(jnp.concatenate(
                    [ds.reshape(BLK, BLK).astype(BF), prob.reshape(BLK, BLK).astype(BF)], axis=1))
            both = jnp.concatenate(pieces, axis=0)
            dkv = jnp.dot(both, qd2[k], preferred_element_type=F32)
            for u in range(width):
                parts[i * SLOTS + e + u] = dkv[u * BLK:(u + 1) * BLK].astype(BF)
            keys = jnp.concatenate([kvt_ref[slots[e + u]] for u in range(width)], axis=1)
            term = jnp.dot(keys, both, preferred_element_type=F32)
            term = (term[0:HDIM, 0:BLK], term[HDIM:, BLK:])
            mixed = term if mixed is None else (mixed[0] + term[0], mixed[1] + term[1])
        yield True
        od_ref[i] = jnp.concatenate([mixed[0] * 0.125, mixed[1]], axis=0).T.astype(BF)

    @pl.loop(0, HALF // 2)
    def _(t):
        i0 = 2 * ((mine // 2 - t + 8) % 8)
        for k in range(2):
            @pl.when(jnp.logical_not(is_self(i0 + k)))
            def _():
                qd_copy(i0 + k, i0 + k).wait_recv()

        @pl.when(t == 3)
        def _():
            @pl.loop(1, 4)
            def _(u):
                cot_across(x, (x + u) % 4).wait_recv()
                cot_beside((x + u) % 4, c).start()

        runs = [attend(i0 + k, k) for k in range(2)]
        while runs:
            runs = [run for run in runs if next(run, None)]
        for k in range(2):
            i = i0 + k

            @pl.when(jnp.logical_not(is_self(i)))
            def _():
                a_copy(i, mine).start()

            @pl.when(is_self(i))
            def _():
                ret_a[mine] = od_ref[i]

    def gathered(key):
        whole = None
        for i in range(HALF):
            part = parts[jnp.clip(table_s[key, 2 * i + c], 0, TILES)].astype(F32)
            whole = part if whole is None else whole + part
        return whole

    @pl.loop(0, 4)
    def _(t):
        r = (t + s // 8) % 4

        @pl.loop(0, 4)
        def _(u):
            j = r * 4 + u
            sib_out[j] = gathered(2 * j + 1 - c).astype(BF)

        s_copy(r).start()

    def back_chunk(t):
        r = (t + s // 8) % 4
        s_copy(r).wait_recv()

        @pl.loop(0, 4)
        def _(u):
            j = r * 4 + u
            send_b[j] = (gathered(2 * j + c) + sib[j].astype(F32)).astype(BF)

            @pl.when(jnp.logical_not(is_self(j)))
            def _():
                b_copy(j, mine).start()

            @pl.when(is_self(j))
            def _():
                ret_b[mine] = send_b[j]

    @pl.loop(0, HEADS // 2)
    def _(t):
        pair = (t + s // 4) % (HEADS // 2)
        cols = pl.ds(pl.multiple_of(pair * 128, 128), 128)
        for e in range(2):
            @pl.when(jnp.logical_not(is_self(pair * 2 + e)))
            def _():
                a_copy(pair * 2 + e, pair * 2 + e).wait_recv()

        a0 = ret_a[pair * 2]
        a1 = ret_a[pair * 2 + 1]
        at = jnp.concatenate([a0[:, 64:], a1[:, 64:]], axis=1)
        tiles[pair] = at

        @pl.when(pair != dp)
        def _():
            g_copy(pair, dp).start()

        @pl.when(pair == dp)
        def _():
            group[dp] = at

        dq_ref[:, cols] = jnp.concatenate([a0[:, 0:64], a1[:, 0:64]], axis=1)
        flat[:, cols] = at

    @pl.loop(0, 2)
    def _(t):
        back_chunk(t)

    cot_beside(x, 1 - c).wait_recv()

    @pl.loop(1, 4)
    def _(u):
        cot_beside((x + u) % 4, 1 - c).wait_recv()

    @pl.loop(0, SCENES)
    def _(p):
        @pl.when(p != dp)
        def _():
            g_copy(p, p).wait_recv()

    att = jnp.concatenate([group[p].T for p in range(SCENES)], axis=1)
    for q in range(4):
        grads = jnp.concatenate([cot_ref[p, :, q * 256:(q + 1) * 256] for p in range(SCENES)], axis=0)
        part = jnp.dot(att, grads, preferred_element_type=F32).astype(BF)
        for r in range(8):
            send_y[r * 4 + q] = part[r * 16:(r + 1) * 16]

    @pl.loop(1, 4)
    def _(t):
        y_copy((y + t) % 4, y).start()

    recv_y[y] = send_y[pl.ds(y * 8, 8)]

    @pl.loop(2, 4)
    def _(t):
        back_chunk(t)

    @pl.loop(1, 4)
    def _(t):
        k = (y + 4 - t) % 4
        y_copy(k, k).wait_recv()

    for k in range(8):
        send_z[k] = (recv_y[0, k].astype(F32) + recv_y[1, k].astype(F32) + recv_y[2, k].astype(F32)
                     + recv_y[3, k].astype(F32)).astype(BF)

    @pl.loop(1, 8)
    def _(t):
        z_copy((z + t) % 8, z).start()

    recv_z[z] = send_z[z]

    @pl.loop(0, 4)
    def _(t):
        cols = pl.ds(pl.multiple_of(t * 256, 256), 256)
        o_ref[:, cols] = jnp.dot(flat[...], w_ref[:, cols], preferred_element_type=F32).astype(BF)

    @pl.loop(1, 8)
    def _(t):
        k = (z + 8 - t) % 8
        z_copy(k, k).wait_recv()

    whole = recv_z[0].astype(F32)
    for k in range(1, 8):
        whole = whole + recv_z[k].astype(F32)
    mine_w[...] = whole * (SCENES * NB * BLK) ** (-0.5)
    keeps = 4 * dp + s // 8 == s

    @pl.loop(0, SCENES)
    def _(t):
        p = (dp + t) % SCENES
        local_end = jnp.logical_and(t == 0, keeps)

        @pl.when(jnp.logical_not(local_end))
        def _():
            f_copy(p, s % 8).start()

        @pl.when(local_end)
        def _():
            stage[s % 8] = mine_w[...]

    @pl.loop(0, HEADS // 2)
    def _(pair):
        cols = pl.ds(pl.multiple_of(pair * 128, 128), 128)
        for e in range(2):
            @pl.when(jnp.logical_not(is_self(pair * 2 + e)))
            def _():
                b_copy(pair * 2 + e, pair * 2 + e).wait_recv()

        a0 = ret_b[pair * 2]
        a1 = ret_b[pair * 2 + 1]
        dk_ref[:, cols] = jnp.concatenate([a0[:, 0:64], a1[:, 0:64]], axis=1)
        dv_ref[:, cols] = jnp.concatenate([a0[:, 64:], a1[:, 64:]], axis=1)

    @pl.loop(0, SCENES)
    def _(t):
        @pl.when(jnp.logical_not(jnp.logical_and(s // 4 == dp, 8 * (s % 4) + t == s)))
        def _():
            f_copy(dp, t).wait_recv()

    for t in range(SCENES):
        wg_ref[16 * (t // 4):16 * (t // 4) + 16, 256 * (t % 4):256 * (t % 4) + 256] = stage[t]

    @pl.loop(0, HALF)
    def _(j):
        relay(j, c).wait_send()

        @pl.when(jnp.logical_not(is_self(j)))
        def _():
            kv_copy(j, s, mine).wait_send()
            qd_copy(j, mine).wait_send()
            a_copy(j, mine).wait_send()
            b_copy(j, mine).wait_send()

    @pl.loop(0, 4)
    def _(r):
        s_copy(r).wait_send()
        cot_beside(r, c).wait_send()

        @pl.when(r != x)
        def _():
            cot_across(r, x).wait_send()

    @pl.loop(0, SCENES)
    def _(t):
        p = (dp + t) % SCENES

        @pl.when(t != 0)
        def _():
            g_copy(p, dp).wait_send()

        @pl.when(jnp.logical_not(jnp.logical_and(t == 0, keeps)))
        def _():
            f_copy(p, s % 8).wait_send()

    @pl.loop(1, 4)
    def _(t):
        y_copy((y + t) % 4, y).wait_send()

    @pl.loop(1, 8)
    def _(t):
        z_copy((z + t) % 8, z).wait_send()


def local(node_queries, node_keys, node_values, cotangent, w_out, neighbours, contacts, ownership):
    flat = jax.ShapeDtypeStruct((BLK, DIM), BF)
    dma = pltpu.SemaphoreType.DMA
    rows = VMEM((BLK, DIM), BF)
    wide = lambda n, t=BF: VMEM((n, BLK, BLK), t)
    vmem = pl.BlockSpec(memory_space=VMEM)
    output, dq, dk, dv, weight_grad = pl.pallas_call(
        fused_kernel,
        out_shape=(flat,) * 4 + (jax.ShapeDtypeStruct((NB, DIM), F32),),
        in_specs=[pl.BlockSpec(memory_space=pltpu.HBM)] * 5 + [vmem] * 3,
        out_specs=(vmem,) * 5,
        scratch_shapes=[
            rows, rows, rows, VMEM((DIM, DIM), BF), VMEM((SCENES, BLK, DIM), BF),
            wide(HALF), wide(HALF), wide(NB), wide(NB), wide(HALF),
            VMEM((BLK, BLK), jnp.int32), VMEM((BLK, BLK), jnp.int32), VMEM((64, BLK), jnp.int32), pltpu.SMEM((64, BLK), jnp.int32),
            wide(2 * SLOTS, F32), wide(2 * SLOTS, F32), VMEM((2, 2 * BLK, BLK), BF), VMEM((2, BLK, 2 * BLK), BF),
            wide(TILES + 1), wide(HALF), wide(HALF),
            wide(HALF), wide(HALF), wide(HALF), wide(HALF), wide(SCENES), wide(SCENES), rows,
            VMEM((NB, 16, 256), BF), VMEM((4, 8, 16, 256), BF), VMEM((8, 16, 256), BF), VMEM((8, 16, 256), BF),
            VMEM((16, 256), F32), VMEM((SCENES, 16, 256), F32),
            dma((5,)), dma((HALF,)), dma((HALF,)), dma((HALF,)), dma((HALF,)), dma((HALF,)), dma((HALF,)), dma, dma, dma,
            dma((4,)), dma((4,)), dma((4,)), dma((4,)),
            dma((HALF,)), dma((HALF,)), dma((HALF,)), dma((HALF,)), dma((4,)), dma((4,)),
            dma((SCENES,)), dma((SCENES,)), dma((4,)), dma((4,)), dma((8,)), dma((8,)), dma((SCENES,)), dma((SCENES,)),
        ],
        compiler_params=pltpu.CompilerParams(
            collective_id=0, has_side_effects=True, vmem_limit_bytes=48 * 2**20),
        name="sublayer",
    )(node_queries[0], node_keys[0], node_values[0], cotangent[0], w_out, neighbours[0], contacts[0], ownership)
    return (output[None], dq[None], dk[None], dv[None], weight_grad)


def solution(mesh):
    placed = (
        P("dp", "seq", None), P("dp", "seq", None), P("dp", "seq", None), P("dp", "seq", None),
        P(), P("dp", None, None), P("dp", None, None), P("dp", None),
    )
    return jax.shard_map(
        local,
        mesh=mesh,
        in_specs=placed,
        out_specs=(
            P("dp", "seq", None), P("dp", "seq", None), P("dp", "seq", None), P("dp", "seq", None),
            P("seq", None),
        ),
        check_vma=False,
    )
```

```python
import functools

import jax
import jax.numpy as jnp
from jax import lax
from jax.experimental import pallas as pl
from jax.experimental.pallas import tpu as pltpu
from jax.sharding import PartitionSpec as P

HEADS = 16
HDIM = 64
BLK = 128
NB = 32
SCENES = 8
HALF = 16
SLOTS = 13
TILES = HALF * SLOTS
DIM = HEADS * HDIM
MESH = pl.DeviceIdType.MESH
VMEM = pltpu.VMEM
BF = jnp.bfloat16
F32 = jnp.float32


def place():
    dp = lax.axis_index("dp")
    s = lax.axis_index("seq")
    return dp // 2, dp % 2, s


def partner(x, c, s, j):
    return (x * 2 + s % 2, 2 * j + c)


def greet_all(x, c, s):
    barrier = pltpu.get_barrier_semaphore()
    alone = c == s % 2
    dp = x * 2 + c

    def hello(device):
        pl.semaphore_signal(barrier, inc=1, device_id=device, device_id_type=MESH)

    @pl.loop(0, HALF)
    def _(j):
        @pl.when(jnp.logical_not(jnp.logical_and(alone, j == s // 2)))
        def _():
            hello(partner(x, c, s, j))

    @pl.loop(1, SCENES)
    def _(t):
        hello(((dp + t) % SCENES, s))

    y, z = s // 8, s % 8

    @pl.loop(1, 4)
    def _(t):
        hello((dp, (y + t) % 4 * 8 + z))

    @pl.loop(1, 8)
    def _(t):
        hello((dp, y * 8 + (z + t) % 8))

    owner = s // 4

    @pl.loop(0, SCENES)
    def _(t):
        k = 8 * (s % 4) + t

        @pl.when(jnp.logical_not(jnp.logical_and(owner == dp, k == s)))
        def _():
            hello((owner, k))


def await_all(x, c, s):
    barrier = pltpu.get_barrier_semaphore()
    alone = c == s % 2
    keeps = 4 * (x * 2 + c) + s // 8 == s
    total = HALF + SCENES - 1 + 3 + 7 + SCENES
    pl.semaphore_wait(barrier, total - jnp.where(alone, 1, 0) - jnp.where(keeps, 1, 0))


def fused_kernel(
    q_hbm, k_hbm, v_hbm, cot_hbm, w_hbm, near_ref, touch_ref, own_ref,
    o_ref, dq_ref, dk_ref, dv_ref, wg_ref,
    q_ref, k_ref, v_ref, w_ref, cot_ref,
    send_kv, send_qd, kv_ref, kvt_ref, qd_ref,
    lists, lists_sib, table, table_s,
    sbuf, pbuf, qd2, qd2t, parts, od_ref, sib_out,
    ret_a, ret_b, sib, send_b, tiles, group, flat, send_y, recv_y, send_z, recv_z, mine_w, stage,
    in_s, kv_ss, kv_rs, qd_ss, qd_rs, re_ss, re_rs, tb_ss, tb_rs, ts_s, cx_ss, cx_rs, cc_ss, cc_rs,
    a_ss, a_rs, b_ss, b_rs, s_ss, s_rs, g_ss, g_rs, y_ss, y_rs, z_ss, z_rs, f_ss, f_rs,
):
    x, c, s = place()
    dp = x * 2 + c
    y, z = s // 8, s % 8
    alone = c == s % 2
    mine = s // 2
    sibling = (x * 2 + 1 - c, s)

    loads = [
        pltpu.make_async_copy(src, dst, in_s.at[n])
        for n, (src, dst) in enumerate(
            ((k_hbm, k_ref), (v_hbm, v_ref), (cot_hbm, cot_ref.at[dp]), (w_hbm, w_ref), (q_hbm, q_ref)))
    ]
    for load in loads:
        load.start()
    greet_all(x, c, s)

    def is_self(j):
        return jnp.logical_and(alone, j == mine)

    def remote(src, dst, send, recv, device):
        return pltpu.make_async_remote_copy(
            src_ref=src, dst_ref=dst, send_sem=send, recv_sem=recv, device_id=device, device_id_type=MESH)

    def kv_copy(j, block, slot):
        return remote(send_kv.at[j], kv_ref.at[block], kv_ss.at[j], kv_rs.at[slot], partner(x, c, s, j))

    def qd_copy(j, slot):
        return remote(send_qd.at[j], qd_ref.at[slot], qd_ss.at[j], qd_rs.at[slot], partner(x, c, s, j))

    def relay(j, odd):
        return remote(kv_ref.at[2 * j + odd], kv_ref.at[2 * j + odd], re_ss.at[j], re_rs.at[j], sibling)

    def cot_across(other, source):
        return remote(cot_ref.at[source * 2 + c], cot_ref.at[source * 2 + c], cx_ss.at[other], cx_rs.at[source],
                      (other * 2 + c, s))

    def cot_beside(source, core):
        return remote(cot_ref.at[source * 2 + core], cot_ref.at[source * 2 + core], cc_ss.at[source], cc_rs.at[source],
                      sibling)

    def a_copy(j, slot):
        return remote(od_ref.at[j], ret_a.at[slot], a_ss.at[j], a_rs.at[slot], partner(x, c, s, j))

    def b_copy(j, slot):
        return remote(send_b.at[j], ret_b.at[slot], b_ss.at[j], b_rs.at[slot], partner(x, c, s, j))

    def s_copy(r):
        return remote(sib_out.at[pl.ds(r * 4, 4)], sib.at[pl.ds(r * 4, 4)], s_ss.at[r], s_rs.at[r], sibling)

    def g_copy(p, slot):
        return remote(tiles.at[p], group.at[slot], g_ss.at[p], g_rs.at[slot], (p, s))

    def y_copy(k, slot):
        return remote(send_y.at[pl.ds(k * 8, 8)], recv_y.at[slot], y_ss.at[k], y_rs.at[slot], (dp, k * 8 + z))

    def z_copy(k, slot):
        return remote(send_z.at[k], recv_z.at[slot], z_ss.at[k], z_rs.at[slot], (dp, y * 8 + k))

    def f_copy(p, slot):
        return remote(mine_w, stage.at[slot], f_ss.at[p], f_rs.at[slot], (p, 4 * dp + s // 8))

    lists[...] = jnp.full((BLK, BLK), -1, jnp.int32)
    lists[0:NB, 0:4] = near_ref[...]
    lists[0:NB, 4:12] = touch_ref[...]
    lists[NB:NB + 1, 0:NB] = own_ref[...]
    loads[0].wait()
    loads[1].wait()

    @pl.loop(0, HEADS // 2)
    def _(t):
        pair = (t + s // 4) % (HEADS // 2)
        cols = pl.ds(pl.multiple_of(pair * 128, 128), 128)
        k = k_ref[:, cols]
        v = v_ref[:, cols]
        for e in range(2):
            j = pair * 2 + e
            send_kv[j] = jnp.concatenate([k[:, e * 64:e * 64 + 64], v[:, e * 64:e * 64 + 64]], axis=1)

    await_all(x, c, s)
    list_copy = remote(lists, lists_sib, tb_ss, tb_rs, sibling)
    list_copy.start()

    @pl.loop(0, HALF)
    def _(t):
        j = (t + s // 4 * 2) % HALF

        @pl.when(jnp.logical_not(is_self(j)))
        def _():
            kv_copy(j, s, mine).start()

        @pl.when(is_self(j))
        def _():
            kv_ref[s] = send_kv[j]

    for load in loads[2:]:
        load.wait()

    @pl.loop(0, HEADS // 2)
    def _(t):
        pair = (t + s // 4) % (HEADS // 2)
        cols = pl.ds(pl.multiple_of(pair * 128, 128), 128)
        q = q_ref[:, cols] * jnp.asarray(0.125, BF)
        d = lax.dot_general(cot_ref[dp], w_ref[cols, :], (((1,), (1,)), ((), ())),
                            preferred_element_type=F32).astype(BF)
        for e in range(2):
            j = pair * 2 + e
            send_qd[j] = jnp.concatenate([q[:, e * 64:e * 64 + 64], d[:, e * 64:e * 64 + 64]], axis=1)

            @pl.when(jnp.logical_not(is_self(j)))
            def _():
                qd_copy(j, mine).start()

            @pl.when(is_self(j))
            def _():
                qd_ref[mine] = send_qd[j]

    cot_beside(x, c).start()

    @pl.loop(1, 4)
    def _(t):
        cot_across((x + t) % 4, x).start()

    list_copy.wait()
    own = jnp.broadcast_to(alone.astype(jnp.int32), (BLK, BLK))
    chosen = lists[...] * own + lists_sib[...] * (1 - own)
    turned = chosen.T
    key_id = lax.broadcasted_iota(jnp.int32, (NB, BLK), 0)
    block_id = lax.broadcasted_iota(jnp.int32, (NB, BLK), 1)
    lane = lax.broadcasted_iota(jnp.int32, (1, BLK), 1)
    first = block_id // 2 * SLOTS
    owner_row = jnp.broadcast_to(chosen[NB:NB + 1, :], (NB, BLK))
    owner_col = jnp.broadcast_to(turned[0:NB, NB:NB + 1], (NB, BLK))
    pos = jnp.where(key_id == block_id, first, TILES)
    table[NB:NB + 1, :] = lane
    table[NB + 16:NB + 17, :] = jnp.ones((1, BLK), jnp.int32)
    for e in range(12):
        entry = turned[e:e + 1, :]
        match = jnp.broadcast_to(entry, (NB, BLK)) == key_id
        if e >= 4:
            match = jnp.logical_and(match, owner_row != owner_col)
        valid = jnp.max(jnp.where(match, 1, 0), axis=0, keepdims=True)
        pos = jnp.where(match, first + (e + 1), pos)
        table[NB + 1 + e:NB + 2 + e, :] = jnp.where(valid > 0, entry, lane)
        table[NB + 17 + e:NB + 18 + e, :] = valid
    table[0:NB, :] = pos
    to_scalar = pltpu.make_async_copy(table, table_s, ts_s)
    to_scalar.start()
    to_scalar.wait()

    qd2[...] = jnp.zeros((2, 2 * BLK, BLK), BF)
    qd2t[...] = jnp.zeros((2, BLK, 2 * BLK), BF)
    parts[TILES] = jnp.zeros((BLK, BLK), BF)

    @pl.loop(0, HALF)
    def _(t):
        j = (t + mine) % HALF

        @pl.when(jnp.logical_not(is_self(j)))
        def _():
            kv_copy(j, 2 * j + c, j).wait_recv()

        relay(j, c).start()
        kvt_ref[2 * j + c] = kv_ref[2 * j + c].T

    @pl.loop(0, HALF)
    def _(t):
        j = (t + mine) % HALF
        relay(j, 1 - c).wait_recv()
        kvt_ref[2 * j + 1 - c] = kv_ref[2 * j + 1 - c].T

    def fold(part):
        return part.reshape(BLK // 8, 8, BLK)

    spans = [(e, min(2, SLOTS - e)) for e in range(0, SLOTS, 2)]

    def attend(i, k):
        b = 2 * i + c
        slots = [jnp.clip(table_s[NB + e, b], 0, NB - 1) for e in range(SLOTS)]
        qd = qd_ref[i]
        qdt = qd.T
        qd2[k, 0:BLK, 0:HDIM] = qd[:, 0:HDIM]
        qd2[k, BLK:, HDIM:] = qd[:, HDIM:]
        qd2t[k, 0:HDIM, 0:BLK] = qdt[0:HDIM, :]
        qd2t[k, HDIM:, BLK:] = qdt[HDIM:, :]
        yield True
        m = None
        for e, width in spans:
            keys = jnp.concatenate([kv_ref[slots[e + u]] for u in range(width)], axis=0)
            both = jnp.dot(keys, qd2t[k], preferred_element_type=F32)
            for u in range(width):
                part = both[u * BLK:(u + 1) * BLK, 0:BLK]
                if e + u > 0:
                    part = part + (table_s[NB + 16 + e + u, b] - 1).astype(F32) * 1e30
                sbuf[k * SLOTS + e + u] = part
                pbuf[k * SLOTS + e + u] = both[u * BLK:(u + 1) * BLK, BLK:]
                top = jnp.max(fold(part), axis=0)
                m = top if m is None else jnp.maximum(m, top)
        m = jnp.broadcast_to(jnp.max(m, axis=0, keepdims=True), (8, BLK))
        yield True
        total = jnp.zeros((8, BLK), F32)
        dot = jnp.zeros((8, BLK), F32)
        for e in range(SLOTS):
            part = jnp.exp(fold(sbuf[k * SLOTS + e]) - m[None])
            sbuf[k * SLOTS + e] = part.reshape(BLK, BLK)
            total = total + jnp.sum(part, axis=0)
            dot = dot + jnp.sum(part * fold(pbuf[k * SLOTS + e]), axis=0)
        yield True
        inv = 1.0 / jnp.sum(total, axis=0, keepdims=True)
        delta = jnp.broadcast_to(jnp.sum(dot, axis=0, keepdims=True) * inv, (8, BLK))
        inv = jnp.broadcast_to(inv, (8, BLK))
        mixed = None
        for e, width in spans:
            pieces = []
            for u in range(width):
                prob = fold(sbuf[k * SLOTS + e + u]) * inv[None]
                ds = prob * (fold(pbuf[k * SLOTS + e + u]) - delta[None])
                pieces.append(jnp.concatenate(
                    [ds.reshape(BLK, BLK).astype(BF), prob.reshape(BLK, BLK).astype(BF)], axis=1))
            both = jnp.concatenate(pieces, axis=0)
            dkv = jnp.dot(both, qd2[k], preferred_element_type=F32)
            for u in range(width):
                parts[i * SLOTS + e + u] = dkv[u * BLK:(u + 1) * BLK].astype(BF)
            keys = jnp.concatenate([kvt_ref[slots[e + u]] for u in range(width)], axis=1)
            term = jnp.dot(keys, both, preferred_element_type=F32)
            term = (term[0:HDIM, 0:BLK], term[HDIM:, BLK:])
            mixed = term if mixed is None else (mixed[0] + term[0], mixed[1] + term[1])
        yield True
        od_ref[i] = jnp.concatenate([mixed[0] * 0.125, mixed[1]], axis=0).T.astype(BF)

    @pl.loop(0, HALF // 2)
    def _(t):
        i0 = 2 * ((mine // 2 - t + 8) % 8)
        for k in range(2):
            @pl.when(jnp.logical_not(is_self(i0 + k)))
            def _():
                qd_copy(i0 + k, i0 + k).wait_recv()

        @pl.when(t == 3)
        def _():
            @pl.loop(1, 4)
            def _(u):
                cot_across(x, (x + u) % 4).wait_recv()
                cot_beside((x + u) % 4, c).start()

        runs = [attend(i0 + k, k) for k in range(2)]
        while runs:
            runs = [run for run in runs if next(run, None)]
        for k in range(2):
            i = i0 + k

            @pl.when(jnp.logical_not(is_self(i)))
            def _():
                a_copy(i, mine).start()

            @pl.when(is_self(i))
            def _():
                ret_a[mine] = od_ref[i]

    def gathered(key):
        whole = None
        for i in range(HALF):
            part = parts[jnp.clip(table_s[key, 2 * i + c], 0, TILES)].astype(F32)
            whole = part if whole is None else whole + part
        return whole

    @pl.loop(0, 4)
    def _(t):
        r = (t + s // 8) % 4

        @pl.loop(0, 4)
        def _(u):
            j = r * 4 + u
            sib_out[j] = gathered(2 * j + 1 - c).astype(BF)

        s_copy(r).start()

    def back_chunk(t):
        r = (t + s // 8) % 4
        s_copy(r).wait_recv()

        @pl.loop(0, 4)
        def _(u):
            j = r * 4 + u
            send_b[j] = (gathered(2 * j + c) + sib[j].astype(F32)).astype(BF)

            @pl.when(jnp.logical_not(is_self(j)))
            def _():
                b_copy(j, mine).start()

            @pl.when(is_self(j))
            def _():
                ret_b[mine] = send_b[j]

    @pl.loop(0, HEADS // 2)
    def _(t):
        pair = (t + s // 4) % (HEADS // 2)
        cols = pl.ds(pl.multiple_of(pair * 128, 128), 128)
        for e in range(2):
            @pl.when(jnp.logical_not(is_self(pair * 2 + e)))
            def _():
                a_copy(pair * 2 + e, pair * 2 + e).wait_recv()

        a0 = ret_a[pair * 2]
        a1 = ret_a[pair * 2 + 1]
        at = jnp.concatenate([a0[:, 64:], a1[:, 64:]], axis=1)
        tiles[pair] = at

        @pl.when(pair != dp)
        def _():
            g_copy(pair, dp).start()

        @pl.when(pair == dp)
        def _():
            group[dp] = at

        dq_ref[:, cols] = jnp.concatenate([a0[:, 0:64], a1[:, 0:64]], axis=1)
        flat[:, cols] = at

    back_chunk(0)

    cot_beside(x, 1 - c).wait_recv()

    @pl.loop(1, 4)
    def _(u):
        cot_beside((x + u) % 4, 1 - c).wait_recv()

    @pl.loop(0, SCENES)
    def _(p):
        @pl.when(p != dp)
        def _():
            g_copy(p, p).wait_recv()

    att = jnp.concatenate([group[p].T for p in range(SCENES)], axis=1)
    for q in range(4):
        grads = jnp.concatenate([cot_ref[p, :, q * 256:(q + 1) * 256] for p in range(SCENES)], axis=0)
        part = jnp.dot(att, grads, preferred_element_type=F32).astype(BF)
        for r in range(8):
            send_y[r * 4 + q] = part[r * 16:(r + 1) * 16]

    @pl.loop(1, 4)
    def _(t):
        y_copy((y + t) % 4, y).start()

    recv_y[y] = send_y[pl.ds(y * 8, 8)]

    back_chunk(1)

    @pl.loop(1, 4)
    def _(t):
        k = (y + 4 - t) % 4
        y_copy(k, k).wait_recv()

    for k in range(8):
        send_z[k] = (recv_y[0, k].astype(F32) + recv_y[1, k].astype(F32) + recv_y[2, k].astype(F32)
                     + recv_y[3, k].astype(F32)).astype(BF)

    @pl.loop(1, 8)
    def _(t):
        z_copy((z + t) % 8, z).start()

    recv_z[z] = send_z[z]
    back_chunk(2)

    @pl.loop(0, 4)
    def _(t):
        cols = pl.ds(pl.multiple_of(t * 256, 256), 256)
        o_ref[:, cols] = jnp.dot(flat[...], w_ref[:, cols], preferred_element_type=F32).astype(BF)

    @pl.loop(1, 8)
    def _(t):
        k = (z + 8 - t) % 8
        z_copy(k, k).wait_recv()

    whole = recv_z[0].astype(F32)
    for k in range(1, 8):
        whole = whole + recv_z[k].astype(F32)
    mine_w[...] = whole * (SCENES * NB * BLK) ** (-0.5)
    keeps = 4 * dp + s // 8 == s

    @pl.loop(0, SCENES)
    def _(t):
        p = (dp + t) % SCENES
        local_end = jnp.logical_and(t == 0, keeps)

        @pl.when(jnp.logical_not(local_end))
        def _():
            f_copy(p, s % 8).start()

        @pl.when(local_end)
        def _():
            stage[s % 8] = mine_w[...]

    back_chunk(3)

    @pl.loop(0, HEADS // 2)
    def _(pair):
        cols = pl.ds(pl.multiple_of(pair * 128, 128), 128)
        for e in range(2):
            @pl.when(jnp.logical_not(is_self(pair * 2 + e)))
            def _():
                b_copy(pair * 2 + e, pair * 2 + e).wait_recv()

        a0 = ret_b[pair * 2]
        a1 = ret_b[pair * 2 + 1]
        dk_ref[:, cols] = jnp.concatenate([a0[:, 0:64], a1[:, 0:64]], axis=1)
        dv_ref[:, cols] = jnp.concatenate([a0[:, 64:], a1[:, 64:]], axis=1)

    @pl.loop(0, SCENES)
    def _(t):
        @pl.when(jnp.logical_not(jnp.logical_and(s // 4 == dp, 8 * (s % 4) + t == s)))
        def _():
            f_copy(dp, t).wait_recv()

    for t in range(SCENES):
        wg_ref[16 * (t // 4):16 * (t // 4) + 16, 256 * (t % 4):256 * (t % 4) + 256] = stage[t]

    @pl.loop(0, HALF)
    def _(j):
        relay(j, c).wait_send()

        @pl.when(jnp.logical_not(is_self(j)))
        def _():
            kv_copy(j, s, mine).wait_send()
            qd_copy(j, mine).wait_send()
            a_copy(j, mine).wait_send()
            b_copy(j, mine).wait_send()

    @pl.loop(0, 4)
    def _(r):
        s_copy(r).wait_send()
        cot_beside(r, c).wait_send()

        @pl.when(r != x)
        def _():
            cot_across(r, x).wait_send()

    @pl.loop(0, SCENES)
    def _(t):
        p = (dp + t) % SCENES

        @pl.when(t != 0)
        def _():
            g_copy(p, dp).wait_send()

        @pl.when(jnp.logical_not(jnp.logical_and(t == 0, keeps)))
        def _():
            f_copy(p, s % 8).wait_send()

    @pl.loop(1, 4)
    def _(t):
        y_copy((y + t) % 4, y).wait_send()

    @pl.loop(1, 8)
    def _(t):
        z_copy((z + t) % 8, z).wait_send()


def local(node_queries, node_keys, node_values, cotangent, w_out, neighbours, contacts, ownership):
    flat = jax.ShapeDtypeStruct((BLK, DIM), BF)
    dma = pltpu.SemaphoreType.DMA
    rows = VMEM((BLK, DIM), BF)
    wide = lambda n, t=BF: VMEM((n, BLK, BLK), t)
    vmem = pl.BlockSpec(memory_space=VMEM)
    output, dq, dk, dv, weight_grad = pl.pallas_call(
        fused_kernel,
        out_shape=(flat,) * 4 + (jax.ShapeDtypeStruct((NB, DIM), F32),),
        in_specs=[pl.BlockSpec(memory_space=pltpu.HBM)] * 5 + [vmem] * 3,
        out_specs=(vmem,) * 5,
        scratch_shapes=[
            rows, rows, rows, VMEM((DIM, DIM), BF), VMEM((SCENES, BLK, DIM), BF),
            wide(HALF), wide(HALF), wide(NB), wide(NB), wide(HALF),
            VMEM((BLK, BLK), jnp.int32), VMEM((BLK, BLK), jnp.int32), VMEM((64, BLK), jnp.int32), pltpu.SMEM((64, BLK), jnp.int32),
            wide(2 * SLOTS, F32), wide(2 * SLOTS, F32), VMEM((2, 2 * BLK, BLK), BF), VMEM((2, BLK, 2 * BLK), BF),
            wide(TILES + 1), wide(HALF), wide(HALF),
            wide(HALF), wide(HALF), wide(HALF), wide(HALF), wide(SCENES), wide(SCENES), rows,
            VMEM((NB, 16, 256), BF), VMEM((4, 8, 16, 256), BF), VMEM((8, 16, 256), BF), VMEM((8, 16, 256), BF),
            VMEM((16, 256), F32), VMEM((SCENES, 16, 256), F32),
            dma((5,)), dma((HALF,)), dma((HALF,)), dma((HALF,)), dma((HALF,)), dma((HALF,)), dma((HALF,)), dma, dma, dma,
            dma((4,)), dma((4,)), dma((4,)), dma((4,)),
            dma((HALF,)), dma((HALF,)), dma((HALF,)), dma((HALF,)), dma((4,)), dma((4,)),
            dma((SCENES,)), dma((SCENES,)), dma((4,)), dma((4,)), dma((8,)), dma((8,)), dma((SCENES,)), dma((SCENES,)),
        ],
        compiler_params=pltpu.CompilerParams(
            collective_id=0, has_side_effects=True, vmem_limit_bytes=53 * 2**20),
        name="sublayer",
    )(node_queries[0], node_keys[0], node_values[0], cotangent[0], w_out, neighbours[0], contacts[0], ownership)
    return (output[None], dq[None], dk[None], dv[None], weight_grad)


def solution(mesh):
    placed = (
        P("dp", "seq", None), P("dp", "seq", None), P("dp", "seq", None), P("dp", "seq", None),
        P(), P("dp", None, None), P("dp", None, None), P("dp", None),
    )
    return jax.shard_map(
        local,
        mesh=mesh,
        in_specs=placed,
        out_specs=(
            P("dp", "seq", None), P("dp", "seq", None), P("dp", "seq", None), P("dp", "seq", None),
            P("seq", None),
        ),
        check_vma=False,
    )
```

```python
import functools

import jax
import jax.numpy as jnp
from jax import lax
from jax.experimental import pallas as pl
from jax.experimental.pallas import tpu as pltpu
from jax.sharding import PartitionSpec as P

HEADS = 16
HDIM = 64
BLK = 128
NB = 32
SCENES = 8
HALF = 16
SLOTS = 13
TILES = HALF * SLOTS
DIM = HEADS * HDIM
MESH = pl.DeviceIdType.MESH
VMEM = pltpu.VMEM
BF = jnp.bfloat16
F32 = jnp.float32


def place():
    dp = lax.axis_index("dp")
    s = lax.axis_index("seq")
    return dp // 2, dp % 2, s


def partner(x, c, s, j):
    return (x * 2 + s % 2, 2 * j + c)


def greet_all(x, c, s):
    barrier = pltpu.get_barrier_semaphore()
    alone = c == s % 2
    dp = x * 2 + c

    def hello(device):
        pl.semaphore_signal(barrier, inc=1, device_id=device, device_id_type=MESH)

    @pl.loop(0, HALF)
    def _(j):
        @pl.when(jnp.logical_not(jnp.logical_and(alone, j == s // 2)))
        def _():
            hello(partner(x, c, s, j))

    @pl.loop(1, SCENES)
    def _(t):
        hello(((dp + t) % SCENES, s))

    y, z = s // 8, s % 8

    @pl.loop(1, 4)
    def _(t):
        hello((dp, (y + t) % 4 * 8 + z))

    @pl.loop(1, 8)
    def _(t):
        hello((dp, y * 8 + (z + t) % 8))

    owner = s // 4

    @pl.loop(0, SCENES)
    def _(t):
        k = 8 * (s % 4) + t

        @pl.when(jnp.logical_not(jnp.logical_and(owner == dp, k == s)))
        def _():
            hello((owner, k))


def await_all(x, c, s):
    barrier = pltpu.get_barrier_semaphore()
    alone = c == s % 2
    keeps = 4 * (x * 2 + c) + s // 8 == s
    total = HALF + SCENES - 1 + 3 + 7 + SCENES
    pl.semaphore_wait(barrier, total - jnp.where(alone, 1, 0) - jnp.where(keeps, 1, 0))


def fused_kernel(
    q_hbm, k_hbm, v_hbm, cot_hbm, w_hbm, near_ref, touch_ref, own_ref,
    o_ref, dq_ref, dk_ref, dv_ref, wg_ref,
    q_ref, k_ref, v_ref, w_ref, cot_ref,
    send_kv, send_qd, kv_ref, kvt_ref, qd_ref,
    lists, lists_sib, table, table_s,
    sbuf, pbuf, qd2, qd2t, parts, od_ref, sib_out,
    ret_a, ret_b, sib, send_b, tiles, group, flat, send_y, recv_y, send_z, recv_z, mine_w, stage,
    in_s, kv_ss, kv_rs, qd_ss, qd_rs, re_ss, re_rs, tb_ss, tb_rs, ts_s, cx_ss, cx_rs, cc_ss, cc_rs,
    a_ss, a_rs, b_ss, b_rs, s_ss, s_rs, g_ss, g_rs, y_ss, y_rs, z_ss, z_rs, f_ss, f_rs,
):
    x, c, s = place()
    dp = x * 2 + c
    y, z = s // 8, s % 8
    alone = c == s % 2
    mine = s // 2
    sibling = (x * 2 + 1 - c, s)

    loads = [
        pltpu.make_async_copy(src, dst, in_s.at[n])
        for n, (src, dst) in enumerate(
            ((k_hbm, k_ref), (v_hbm, v_ref), (cot_hbm, cot_ref.at[dp]), (w_hbm, w_ref), (q_hbm, q_ref)))
    ]
    for load in loads:
        load.start()
    greet_all(x, c, s)

    def is_self(j):
        return jnp.logical_and(alone, j == mine)

    def remote(src, dst, send, recv, device):
        return pltpu.make_async_remote_copy(
            src_ref=src, dst_ref=dst, send_sem=send, recv_sem=recv, device_id=device, device_id_type=MESH)

    def kv_copy(j, block, slot):
        return remote(send_kv.at[j], kv_ref.at[block], kv_ss.at[j], kv_rs.at[slot], partner(x, c, s, j))

    def qd_copy(j, slot):
        return remote(send_qd.at[j], qd_ref.at[slot], qd_ss.at[j], qd_rs.at[slot], partner(x, c, s, j))

    def relay(j, odd):
        return remote(kv_ref.at[2 * j + odd], kv_ref.at[2 * j + odd], re_ss.at[j], re_rs.at[j], sibling)

    def cot_across(other, source):
        return remote(cot_ref.at[source * 2 + c], cot_ref.at[source * 2 + c], cx_ss.at[other], cx_rs.at[source],
                      (other * 2 + c, s))

    def cot_beside(source, core):
        return remote(cot_ref.at[source * 2 + core], cot_ref.at[source * 2 + core], cc_ss.at[source], cc_rs.at[source],
                      sibling)

    def a_copy(j, slot):
        return remote(od_ref.at[j], ret_a.at[slot], a_ss.at[j], a_rs.at[slot], partner(x, c, s, j))

    def b_copy(j, slot):
        return remote(send_b.at[j], ret_b.at[slot], b_ss.at[j], b_rs.at[slot], partner(x, c, s, j))

    def s_copy(r):
        return remote(sib_out.at[pl.ds(r * 4, 4)], sib.at[pl.ds(r * 4, 4)], s_ss.at[r], s_rs.at[r], sibling)

    def g_copy(p, slot):
        return remote(tiles.at[p], group.at[slot], g_ss.at[p], g_rs.at[slot], (p, s))

    def y_copy(k, slot):
        return remote(send_y.at[pl.ds(k * 8, 8)], recv_y.at[slot], y_ss.at[k], y_rs.at[slot], (dp, k * 8 + z))

    def z_copy(k, slot):
        return remote(send_z.at[k], recv_z.at[slot], z_ss.at[k], z_rs.at[slot], (dp, y * 8 + k))

    def f_copy(p, slot):
        return remote(mine_w, stage.at[slot], f_ss.at[p], f_rs.at[slot], (p, 4 * dp + s // 8))

    lists[...] = jnp.full((BLK, BLK), -1, jnp.int32)
    lists[0:NB, 0:4] = near_ref[...]
    lists[0:NB, 4:12] = touch_ref[...]
    lists[NB:NB + 1, 0:NB] = own_ref[...]
    loads[0].wait()
    loads[1].wait()

    @pl.loop(0, HEADS // 2)
    def _(t):
        pair = (t + s // 4) % (HEADS // 2)
        cols = pl.ds(pl.multiple_of(pair * 128, 128), 128)
        k = k_ref[:, cols]
        v = v_ref[:, cols]
        for e in range(2):
            j = pair * 2 + e
            send_kv[j] = jnp.concatenate([k[:, e * 64:e * 64 + 64], v[:, e * 64:e * 64 + 64]], axis=1)

    await_all(x, c, s)
    list_copy = remote(lists, lists_sib, tb_ss, tb_rs, sibling)
    list_copy.start()

    @pl.loop(0, HALF)
    def _(t):
        j = (t + s // 4 * 2) % HALF

        @pl.when(jnp.logical_not(is_self(j)))
        def _():
            kv_copy(j, s, mine).start()

        @pl.when(is_self(j))
        def _():
            kv_ref[s] = send_kv[j]

    for load in loads[2:]:
        load.wait()

    @pl.loop(0, HEADS // 2)
    def _(t):
        pair = (t + s // 4) % (HEADS // 2)
        cols = pl.ds(pl.multiple_of(pair * 128, 128), 128)
        q = q_ref[:, cols] * jnp.asarray(0.125, BF)
        d = lax.dot_general(cot_ref[dp], w_ref[cols, :], (((1,), (1,)), ((), ())),
                            preferred_element_type=F32).astype(BF)
        for e in range(2):
            j = pair * 2 + e
            send_qd[j] = jnp.concatenate([q[:, e * 64:e * 64 + 64], d[:, e * 64:e * 64 + 64]], axis=1)

            @pl.when(jnp.logical_not(is_self(j)))
            def _():
                qd_copy(j, mine).start()

            @pl.when(is_self(j))
            def _():
                qd_ref[mine] = send_qd[j]

    cot_beside(x, c).start()

    @pl.loop(1, 4)
    def _(t):
        cot_across((x + t) % 4, x).start()

    list_copy.wait()
    own = jnp.broadcast_to(alone.astype(jnp.int32), (BLK, BLK))
    chosen = lists[...] * own + lists_sib[...] * (1 - own)
    turned = chosen.T
    key_id = lax.broadcasted_iota(jnp.int32, (NB, BLK), 0)
    block_id = lax.broadcasted_iota(jnp.int32, (NB, BLK), 1)
    lane = lax.broadcasted_iota(jnp.int32, (1, BLK), 1)
    first = block_id // 2 * SLOTS
    owner_row = jnp.broadcast_to(chosen[NB:NB + 1, :], (NB, BLK))
    owner_col = jnp.broadcast_to(turned[0:NB, NB:NB + 1], (NB, BLK))
    pos = jnp.where(key_id == block_id, first, TILES)
    table[NB:NB + 1, :] = lane
    table[NB + 16:NB + 17, :] = jnp.ones((1, BLK), jnp.int32)
    for e in range(12):
        entry = turned[e:e + 1, :]
        match = jnp.broadcast_to(entry, (NB, BLK)) == key_id
        if e >= 4:
            match = jnp.logical_and(match, owner_row != owner_col)
        valid = jnp.max(jnp.where(match, 1, 0), axis=0, keepdims=True)
        pos = jnp.where(match, first + (e + 1), pos)
        table[NB + 1 + e:NB + 2 + e, :] = jnp.where(valid > 0, entry, lane)
        table[NB + 17 + e:NB + 18 + e, :] = valid
    table[0:NB, :] = pos
    to_scalar = pltpu.make_async_copy(table, table_s, ts_s)
    to_scalar.start()
    to_scalar.wait()

    qd2[...] = jnp.zeros((2, 2 * BLK, BLK), BF)
    qd2t[...] = jnp.zeros((2, BLK, 2 * BLK), BF)
    parts[TILES] = jnp.zeros((BLK, BLK), BF)

    def relayed(t):
        j = (t + mine) % HALF
        relay(j, 1 - c).wait_recv()
        kvt_ref[2 * j + 1 - c] = kv_ref[2 * j + 1 - c].T

    @pl.loop(0, HALF)
    def _(t):
        j = (t + mine) % HALF

        @pl.when(jnp.logical_not(is_self(j)))
        def _():
            kv_copy(j, 2 * j + c, j).wait_recv()

        relay(j, c).start()
        kvt_ref[2 * j + c] = kv_ref[2 * j + c].T

        @pl.when(t >= 4)
        def _():
            relayed(t - 4)

    @pl.loop(HALF - 4, HALF)
    def _(t):
        relayed(t)

    def fold(part):
        return part.reshape(BLK // 8, 8, BLK)

    spans = [(e, min(2, SLOTS - e)) for e in range(0, SLOTS, 2)]

    def attend(i, k):
        b = 2 * i + c
        slots = [jnp.clip(table_s[NB + e, b], 0, NB - 1) for e in range(SLOTS)]
        qd = qd_ref[i]
        qdt = qd.T
        qd2[k, 0:BLK, 0:HDIM] = qd[:, 0:HDIM]
        qd2[k, BLK:, HDIM:] = qd[:, HDIM:]
        qd2t[k, 0:HDIM, 0:BLK] = qdt[0:HDIM, :]
        qd2t[k, HDIM:, BLK:] = qdt[HDIM:, :]
        yield True
        m = None
        for e, width in spans:
            keys = jnp.concatenate([kv_ref[slots[e + u]] for u in range(width)], axis=0)
            both = jnp.dot(keys, qd2t[k], preferred_element_type=F32)
            for u in range(width):
                part = both[u * BLK:(u + 1) * BLK, 0:BLK]
                if e + u > 0:
                    part = part + (table_s[NB + 16 + e + u, b] - 1).astype(F32) * 1e30
                sbuf[k * SLOTS + e + u] = part
                pbuf[k * SLOTS + e + u] = both[u * BLK:(u + 1) * BLK, BLK:]
                top = jnp.max(fold(part), axis=0)
                m = top if m is None else jnp.maximum(m, top)
        m = jnp.broadcast_to(jnp.max(m, axis=0, keepdims=True), (8, BLK))
        yield True
        total = jnp.zeros((8, BLK), F32)
        dot = jnp.zeros((8, BLK), F32)
        for e in range(SLOTS):
            part = jnp.exp(fold(sbuf[k * SLOTS + e]) - m[None])
            sbuf[k * SLOTS + e] = part.reshape(BLK, BLK)
            total = total + jnp.sum(part, axis=0)
            dot = dot + jnp.sum(part * fold(pbuf[k * SLOTS + e]), axis=0)
        yield True
        inv = 1.0 / jnp.sum(total, axis=0, keepdims=True)
        delta = jnp.broadcast_to(jnp.sum(dot, axis=0, keepdims=True) * inv, (8, BLK))
        inv = jnp.broadcast_to(inv, (8, BLK))
        mixed = None
        for e, width in spans:
            pieces = []
            for u in range(width):
                prob = fold(sbuf[k * SLOTS + e + u]) * inv[None]
                ds = prob * (fold(pbuf[k * SLOTS + e + u]) - delta[None])
                pieces.append(jnp.concatenate(
                    [ds.reshape(BLK, BLK).astype(BF), prob.reshape(BLK, BLK).astype(BF)], axis=1))
            both = jnp.concatenate(pieces, axis=0)
            dkv = jnp.dot(both, qd2[k], preferred_element_type=F32)
            for u in range(width):
                parts[i * SLOTS + e + u] = dkv[u * BLK:(u + 1) * BLK].astype(BF)
            keys = jnp.concatenate([kvt_ref[slots[e + u]] for u in range(width)], axis=1)
            term = jnp.dot(keys, both, preferred_element_type=F32)
            term = (term[0:HDIM, 0:BLK], term[HDIM:, BLK:])
            mixed = term if mixed is None else (mixed[0] + term[0], mixed[1] + term[1])
        yield True
        od_ref[i] = jnp.concatenate([mixed[0] * 0.125, mixed[1]], axis=0).T.astype(BF)

    @pl.loop(0, HALF // 2)
    def _(t):
        i0 = 2 * ((mine // 2 - t + 8) % 8)
        for k in range(2):
            @pl.when(jnp.logical_not(is_self(i0 + k)))
            def _():
                qd_copy(i0 + k, i0 + k).wait_recv()

        @pl.when(t == 3)
        def _():
            @pl.loop(1, 4)
            def _(u):
                cot_across(x, (x + u) % 4).wait_recv()
                cot_beside((x + u) % 4, c).start()

        runs = [attend(i0 + k, k) for k in range(2)]
        while runs:
            runs = [run for run in runs if next(run, None)]
        for k in range(2):
            i = i0 + k

            @pl.when(jnp.logical_not(is_self(i)))
            def _():
                a_copy(i, mine).start()

            @pl.when(is_self(i))
            def _():
                ret_a[mine] = od_ref[i]

    def gathered(key):
        whole = None
        for i in range(HALF):
            part = parts[jnp.clip(table_s[key, 2 * i + c], 0, TILES)].astype(F32)
            whole = part if whole is None else whole + part
        return whole

    @pl.loop(0, 4)
    def _(t):
        r = (t + s // 8) % 4

        @pl.loop(0, 4)
        def _(u):
            j = r * 4 + u
            sib_out[j] = gathered(2 * j + 1 - c).astype(BF)

        s_copy(r).start()

    def back_chunk(t):
        r = (t + s // 8) % 4
        s_copy(r).wait_recv()

        @pl.loop(0, 4)
        def _(u):
            j = r * 4 + u
            send_b[j] = (gathered(2 * j + c) + sib[j].astype(F32)).astype(BF)

            @pl.when(jnp.logical_not(is_self(j)))
            def _():
                b_copy(j, mine).start()

            @pl.when(is_self(j))
            def _():
                ret_b[mine] = send_b[j]

    back_chunk(0)

    @pl.loop(0, HEADS // 2)
    def _(t):
        pair = (t + s // 4) % (HEADS // 2)
        cols = pl.ds(pl.multiple_of(pair * 128, 128), 128)
        for e in range(2):
            @pl.when(jnp.logical_not(is_self(pair * 2 + e)))
            def _():
                a_copy(pair * 2 + e, pair * 2 + e).wait_recv()

        a0 = ret_a[pair * 2]
        a1 = ret_a[pair * 2 + 1]
        at = jnp.concatenate([a0[:, 64:], a1[:, 64:]], axis=1)
        tiles[pair] = at

        @pl.when(pair != dp)
        def _():
            g_copy(pair, dp).start()

        @pl.when(pair == dp)
        def _():
            group[dp] = at

        dq_ref[:, cols] = jnp.concatenate([a0[:, 0:64], a1[:, 0:64]], axis=1)
        flat[:, cols] = at


    cot_beside(x, 1 - c).wait_recv()

    @pl.loop(1, 4)
    def _(u):
        cot_beside((x + u) % 4, 1 - c).wait_recv()

    @pl.loop(0, SCENES)
    def _(p):
        @pl.when(p != dp)
        def _():
            g_copy(p, p).wait_recv()

    att = jnp.concatenate([group[p].T for p in range(SCENES)], axis=1)
    for q in range(4):
        grads = jnp.concatenate([cot_ref[p, :, q * 256:(q + 1) * 256] for p in range(SCENES)], axis=0)
        part = jnp.dot(att, grads, preferred_element_type=F32).astype(BF)
        for r in range(8):
            send_y[r * 4 + q] = part[r * 16:(r + 1) * 16]

    @pl.loop(1, 4)
    def _(t):
        y_copy((y + t) % 4, y).start()

    recv_y[y] = send_y[pl.ds(y * 8, 8)]

    back_chunk(1)

    @pl.loop(1, 4)
    def _(t):
        k = (y + 4 - t) % 4
        y_copy(k, k).wait_recv()

    for k in range(8):
        send_z[k] = (recv_y[0, k].astype(F32) + recv_y[1, k].astype(F32) + recv_y[2, k].astype(F32)
                     + recv_y[3, k].astype(F32)).astype(BF)

    @pl.loop(1, 8)
    def _(t):
        z_copy((z + t) % 8, z).start()

    recv_z[z] = send_z[z]
    back_chunk(2)

    @pl.loop(0, 4)
    def _(t):
        cols = pl.ds(pl.multiple_of(t * 256, 256), 256)
        o_ref[:, cols] = jnp.dot(flat[...], w_ref[:, cols], preferred_element_type=F32).astype(BF)

    @pl.loop(1, 8)
    def _(t):
        k = (z + 8 - t) % 8
        z_copy(k, k).wait_recv()

    whole = recv_z[0].astype(F32)
    for k in range(1, 8):
        whole = whole + recv_z[k].astype(F32)
    mine_w[...] = whole * (SCENES * NB * BLK) ** (-0.5)
    keeps = 4 * dp + s // 8 == s

    @pl.loop(0, SCENES)
    def _(t):
        p = (dp + t) % SCENES
        local_end = jnp.logical_and(t == 0, keeps)

        @pl.when(jnp.logical_not(local_end))
        def _():
            f_copy(p, s % 8).start()

        @pl.when(local_end)
        def _():
            stage[s % 8] = mine_w[...]

    back_chunk(3)

    @pl.loop(0, HEADS // 2)
    def _(pair):
        cols = pl.ds(pl.multiple_of(pair * 128, 128), 128)
        for e in range(2):
            @pl.when(jnp.logical_not(is_self(pair * 2 + e)))
            def _():
                b_copy(pair * 2 + e, pair * 2 + e).wait_recv()

        a0 = ret_b[pair * 2]
        a1 = ret_b[pair * 2 + 1]
        dk_ref[:, cols] = jnp.concatenate([a0[:, 0:64], a1[:, 0:64]], axis=1)
        dv_ref[:, cols] = jnp.concatenate([a0[:, 64:], a1[:, 64:]], axis=1)

    @pl.loop(0, SCENES)
    def _(t):
        @pl.when(jnp.logical_not(jnp.logical_and(s // 4 == dp, 8 * (s % 4) + t == s)))
        def _():
            f_copy(dp, t).wait_recv()

    for t in range(SCENES):
        wg_ref[16 * (t // 4):16 * (t // 4) + 16, 256 * (t % 4):256 * (t % 4) + 256] = stage[t]

    @pl.loop(0, HALF)
    def _(j):
        relay(j, c).wait_send()

        @pl.when(jnp.logical_not(is_self(j)))
        def _():
            kv_copy(j, s, mine).wait_send()
            qd_copy(j, mine).wait_send()
            a_copy(j, mine).wait_send()
            b_copy(j, mine).wait_send()

    @pl.loop(0, 4)
    def _(r):
        s_copy(r).wait_send()
        cot_beside(r, c).wait_send()

        @pl.when(r != x)
        def _():
            cot_across(r, x).wait_send()

    @pl.loop(0, SCENES)
    def _(t):
        p = (dp + t) % SCENES

        @pl.when(t != 0)
        def _():
            g_copy(p, dp).wait_send()

        @pl.when(jnp.logical_not(jnp.logical_and(t == 0, keeps)))
        def _():
            f_copy(p, s % 8).wait_send()

    @pl.loop(1, 4)
    def _(t):
        y_copy((y + t) % 4, y).wait_send()

    @pl.loop(1, 8)
    def _(t):
        z_copy((z + t) % 8, z).wait_send()


def local(node_queries, node_keys, node_values, cotangent, w_out, neighbours, contacts, ownership):
    flat = jax.ShapeDtypeStruct((BLK, DIM), BF)
    dma = pltpu.SemaphoreType.DMA
    rows = VMEM((BLK, DIM), BF)
    wide = lambda n, t=BF: VMEM((n, BLK, BLK), t)
    vmem = pl.BlockSpec(memory_space=VMEM)
    output, dq, dk, dv, weight_grad = pl.pallas_call(
        fused_kernel,
        out_shape=(flat,) * 4 + (jax.ShapeDtypeStruct((NB, DIM), F32),),
        in_specs=[pl.BlockSpec(memory_space=pltpu.HBM)] * 5 + [vmem] * 3,
        out_specs=(vmem,) * 5,
        scratch_shapes=[
            rows, rows, rows, VMEM((DIM, DIM), BF), VMEM((SCENES, BLK, DIM), BF),
            wide(HALF), wide(HALF), wide(NB), wide(NB), wide(HALF),
            VMEM((BLK, BLK), jnp.int32), VMEM((BLK, BLK), jnp.int32), VMEM((64, BLK), jnp.int32), pltpu.SMEM((64, BLK), jnp.int32),
            wide(2 * SLOTS, F32), wide(2 * SLOTS, F32), VMEM((2, 2 * BLK, BLK), BF), VMEM((2, BLK, 2 * BLK), BF),
            wide(TILES + 1), wide(HALF), wide(HALF),
            wide(HALF), wide(HALF), wide(HALF), wide(HALF), wide(SCENES), wide(SCENES), rows,
            VMEM((NB, 16, 256), BF), VMEM((4, 8, 16, 256), BF), VMEM((8, 16, 256), BF), VMEM((8, 16, 256), BF),
            VMEM((16, 256), F32), VMEM((SCENES, 16, 256), F32),
            dma((5,)), dma((HALF,)), dma((HALF,)), dma((HALF,)), dma((HALF,)), dma((HALF,)), dma((HALF,)), dma, dma, dma,
            dma((4,)), dma((4,)), dma((4,)), dma((4,)),
            dma((HALF,)), dma((HALF,)), dma((HALF,)), dma((HALF,)), dma((4,)), dma((4,)),
            dma((SCENES,)), dma((SCENES,)), dma((4,)), dma((4,)), dma((8,)), dma((8,)), dma((SCENES,)), dma((SCENES,)),
        ],
        compiler_params=pltpu.CompilerParams(
            collective_id=0, has_side_effects=True, vmem_limit_bytes=55259136),
        name="sublayer",
    )(node_queries[0], node_keys[0], node_values[0], cotangent[0], w_out, neighbours[0], contacts[0], ownership)
    return (output[None], dq[None], dk[None], dv[None], weight_grad)


def solution(mesh):
    placed = (
        P("dp", "seq", None), P("dp", "seq", None), P("dp", "seq", None), P("dp", "seq", None),
        P(), P("dp", None, None), P("dp", None, None), P("dp", None),
    )
    return jax.shard_map(
        local,
        mesh=mesh,
        in_specs=placed,
        out_specs=(
            P("dp", "seq", None), P("dp", "seq", None), P("dp", "seq", None), P("dp", "seq", None),
            P("seq", None),
        ),
        check_vma=False,
    )
```

```python
import functools

import jax
import jax.numpy as jnp
from jax import lax
from jax.experimental import pallas as pl
from jax.experimental.pallas import tpu as pltpu
from jax.sharding import PartitionSpec as P

HEADS = 16
HDIM = 64
BLK = 128
NB = 32
SCENES = 8
HALF = 16
SLOTS = 13
TILES = HALF * SLOTS
DIM = HEADS * HDIM
MESH = pl.DeviceIdType.MESH
VMEM = pltpu.VMEM
BF = jnp.bfloat16
F32 = jnp.float32


def place():
    dp = lax.axis_index("dp")
    s = lax.axis_index("seq")
    return dp // 2, dp % 2, s


def partner(x, c, s, j):
    return (x * 2 + s % 2, 2 * j + c)


def greet_all(x, c, s):
    barrier = pltpu.get_barrier_semaphore()
    alone = c == s % 2
    dp = x * 2 + c

    def hello(device):
        pl.semaphore_signal(barrier, inc=1, device_id=device, device_id_type=MESH)

    @pl.loop(0, HALF)
    def _(j):
        @pl.when(jnp.logical_not(jnp.logical_and(alone, j == s // 2)))
        def _():
            hello(partner(x, c, s, j))

    @pl.loop(1, SCENES)
    def _(t):
        hello(((dp + t) % SCENES, s))

    y, z = s // 8, s % 8

    @pl.loop(1, 4)
    def _(t):
        hello((dp, (y + t) % 4 * 8 + z))

    @pl.loop(1, 8)
    def _(t):
        hello((dp, y * 8 + (z + t) % 8))

    owner = s // 4

    @pl.loop(0, SCENES)
    def _(t):
        k = 8 * (s % 4) + t

        @pl.when(jnp.logical_not(jnp.logical_and(owner == dp, k == s)))
        def _():
            hello((owner, k))


def await_all(x, c, s):
    barrier = pltpu.get_barrier_semaphore()
    alone = c == s % 2
    keeps = 4 * (x * 2 + c) + s // 8 == s
    total = HALF + SCENES - 1 + 3 + 7 + SCENES
    pl.semaphore_wait(barrier, total - jnp.where(alone, 1, 0) - jnp.where(keeps, 1, 0))


def fused_kernel(
    q_hbm, k_hbm, v_hbm, cot_hbm, w_hbm, near_ref, touch_ref, own_ref,
    o_ref, dq_ref, dk_ref, dv_ref, wg_ref,
    q_ref, k_ref, v_ref, w_ref, cot_ref,
    send_kv, send_qd, kv_ref, kvt_ref, qd_ref,
    lists, lists_sib, table, table_s,
    sbuf, pbuf, qd2, qd2t, parts, od_ref, sib_out,
    ret_a, ret_b, sib, send_b, tiles, group, flat, send_y, recv_y, send_z, recv_z, mine_w, stage,
    in_s, kv_ss, kv_rs, qd_ss, qd_rs, re_ss, re_rs, tb_ss, tb_rs, ts_s, cx_ss, cx_rs, cc_ss, cc_rs,
    a_ss, a_rs, b_ss, b_rs, s_ss, s_rs, g_ss, g_rs, y_ss, y_rs, z_ss, z_rs, f_ss, f_rs,
):
    x, c, s = place()
    dp = x * 2 + c
    y, z = s // 8, s % 8
    alone = c == s % 2
    mine = s // 2
    sibling = (x * 2 + 1 - c, s)

    loads = [
        pltpu.make_async_copy(src, dst, in_s.at[n])
        for n, (src, dst) in enumerate(
            ((k_hbm, k_ref), (v_hbm, v_ref), (cot_hbm, cot_ref.at[dp]), (w_hbm, w_ref), (q_hbm, q_ref)))
    ]
    for load in loads:
        load.start()
    greet_all(x, c, s)

    def is_self(j):
        return jnp.logical_and(alone, j == mine)

    def remote(src, dst, send, recv, device):
        return pltpu.make_async_remote_copy(
            src_ref=src, dst_ref=dst, send_sem=send, recv_sem=recv, device_id=device, device_id_type=MESH)

    def kv_copy(j, block, slot):
        return remote(send_kv.at[j], kv_ref.at[block], kv_ss.at[j], kv_rs.at[slot], partner(x, c, s, j))

    def qd_copy(j, slot):
        return remote(send_qd.at[j], qd_ref.at[slot], qd_ss.at[j], qd_rs.at[slot], partner(x, c, s, j))

    def relay(j, odd):
        return remote(kv_ref.at[2 * j + odd], kv_ref.at[2 * j + odd], re_ss.at[j], re_rs.at[j], sibling)

    def cot_across(other, source):
        return remote(cot_ref.at[source * 2 + c], cot_ref.at[source * 2 + c], cx_ss.at[other], cx_rs.at[source],
                      (other * 2 + c, s))

    def cot_beside(source, core):
        return remote(cot_ref.at[source * 2 + core], cot_ref.at[source * 2 + core], cc_ss.at[source], cc_rs.at[source],
                      sibling)

    def a_copy(j, slot):
        return remote(od_ref.at[j], ret_a.at[slot], a_ss.at[j], a_rs.at[slot], partner(x, c, s, j))

    def b_copy(j, slot):
        return remote(send_b.at[j], ret_b.at[slot], b_ss.at[j], b_rs.at[slot], partner(x, c, s, j))

    def s_copy(r):
        return remote(sib_out.at[pl.ds(r * 4, 4)], sib.at[pl.ds(r * 4, 4)], s_ss.at[r], s_rs.at[r], sibling)

    def g_copy(p, slot):
        return remote(tiles.at[p], group.at[slot], g_ss.at[p], g_rs.at[slot], (p, s))

    def y_copy(k, slot):
        return remote(send_y.at[pl.ds(k * 8, 8)], recv_y.at[slot], y_ss.at[k], y_rs.at[slot], (dp, k * 8 + z))

    def z_copy(k, slot):
        return remote(send_z.at[k], recv_z.at[slot], z_ss.at[k], z_rs.at[slot], (dp, y * 8 + k))

    def f_copy(p, slot):
        return remote(mine_w, stage.at[slot], f_ss.at[p], f_rs.at[slot], (p, 4 * dp + s // 8))

    lists[...] = jnp.full((BLK, BLK), -1, jnp.int32)
    lists[0:NB, 0:4] = near_ref[...]
    lists[0:NB, 4:12] = touch_ref[...]
    lists[NB:NB + 1, 0:NB] = own_ref[...]
    loads[0].wait()
    loads[1].wait()

    @pl.loop(0, HEADS // 2)
    def _(t):
        pair = (t + s // 4) % (HEADS // 2)
        cols = pl.ds(pl.multiple_of(pair * 128, 128), 128)
        k = k_ref[:, cols]
        v = v_ref[:, cols]
        for e in range(2):
            j = pair * 2 + e
            send_kv[j] = jnp.concatenate([k[:, e * 64:e * 64 + 64], v[:, e * 64:e * 64 + 64]], axis=1)

    await_all(x, c, s)
    list_copy = remote(lists, lists_sib, tb_ss, tb_rs, sibling)
    list_copy.start()

    @pl.loop(0, HALF)
    def _(t):
        j = (t + s // 4 * 2) % HALF

        @pl.when(jnp.logical_not(is_self(j)))
        def _():
            kv_copy(j, s, mine).start()

        @pl.when(is_self(j))
        def _():
            kv_ref[s] = send_kv[j]

    for load in loads[2:]:
        load.wait()

    @pl.loop(0, HEADS // 2)
    def _(t):
        pair = (t + s // 4) % (HEADS // 2)
        cols = pl.ds(pl.multiple_of(pair * 128, 128), 128)
        q = q_ref[:, cols] * jnp.asarray(0.125, BF)
        d = lax.dot_general(cot_ref[dp], w_ref[cols, :], (((1,), (1,)), ((), ())),
                            preferred_element_type=F32).astype(BF)
        for e in range(2):
            j = pair * 2 + e
            send_qd[j] = jnp.concatenate([q[:, e * 64:e * 64 + 64], d[:, e * 64:e * 64 + 64]], axis=1)

            @pl.when(jnp.logical_not(is_self(j)))
            def _():
                qd_copy(j, mine).start()

            @pl.when(is_self(j))
            def _():
                qd_ref[mine] = send_qd[j]

    cot_beside(x, c).start()

    @pl.loop(1, 4)
    def _(t):
        cot_across((x + t) % 4, x).start()

    list_copy.wait()
    own = jnp.broadcast_to(alone.astype(jnp.int32), (BLK, BLK))
    chosen = lists[...] * own + lists_sib[...] * (1 - own)
    turned = chosen.T
    key_id = lax.broadcasted_iota(jnp.int32, (NB, BLK), 0)
    block_id = lax.broadcasted_iota(jnp.int32, (NB, BLK), 1)
    lane = lax.broadcasted_iota(jnp.int32, (1, BLK), 1)
    first = block_id // 2 * SLOTS
    owner_row = jnp.broadcast_to(chosen[NB:NB + 1, :], (NB, BLK))
    owner_col = jnp.broadcast_to(turned[0:NB, NB:NB + 1], (NB, BLK))
    pos = jnp.where(key_id == block_id, first, TILES)
    table[NB:NB + 1, :] = lane
    table[NB + 16:NB + 17, :] = jnp.ones((1, BLK), jnp.int32)
    for e in range(12):
        entry = turned[e:e + 1, :]
        match = jnp.broadcast_to(entry, (NB, BLK)) == key_id
        if e >= 4:
            match = jnp.logical_and(match, owner_row != owner_col)
        valid = jnp.max(jnp.where(match, 1, 0), axis=0, keepdims=True)
        pos = jnp.where(match, first + (e + 1), pos)
        table[NB + 1 + e:NB + 2 + e, :] = jnp.where(valid > 0, entry, lane)
        table[NB + 17 + e:NB + 18 + e, :] = valid
    table[0:NB, :] = pos
    to_scalar = pltpu.make_async_copy(table, table_s, ts_s)
    to_scalar.start()
    to_scalar.wait()

    qd2[...] = jnp.zeros((2, 2 * BLK, BLK), BF)
    qd2t[...] = jnp.zeros((2, BLK, 2 * BLK), BF)
    parts[TILES] = jnp.zeros((BLK, BLK), BF)

    @pl.loop(0, HALF)
    def _(t):
        j = (t + mine) % HALF

        @pl.when(jnp.logical_not(is_self(j)))
        def _():
            kv_copy(j, 2 * j + c, j).wait_recv()

        relay(j, c).start()
        kvt_ref[2 * j + c] = kv_ref[2 * j + c].T

    @pl.loop(0, HALF)
    def _(t):
        j = (t + mine) % HALF
        relay(j, 1 - c).wait_recv()
        kvt_ref[2 * j + 1 - c] = kv_ref[2 * j + 1 - c].T

    def fold(part):
        return part.reshape(BLK // 8, 8, BLK)

    spans = [(e, min(2, SLOTS - e)) for e in range(0, SLOTS, 2)]

    def attend(i, k):
        b = 2 * i + c
        slots = [jnp.clip(table_s[NB + e, b], 0, NB - 1) for e in range(SLOTS)]
        qd = qd_ref[i]
        qdt = qd.T
        qd2[k, 0:BLK, 0:HDIM] = qd[:, 0:HDIM]
        qd2[k, BLK:, HDIM:] = qd[:, HDIM:]
        qd2t[k, 0:HDIM, 0:BLK] = qdt[0:HDIM, :]
        qd2t[k, HDIM:, BLK:] = qdt[HDIM:, :]
        yield True
        m = None
        for e, width in spans:
            keys = jnp.concatenate([kv_ref[slots[e + u]] for u in range(width)], axis=0)
            both = jnp.dot(keys, qd2t[k], preferred_element_type=F32)
            for u in range(width):
                part = both[u * BLK:(u + 1) * BLK, 0:BLK]
                if e + u > 0:
                    part = part + (table_s[NB + 16 + e + u, b] - 1).astype(F32) * 1e30
                sbuf[k * SLOTS + e + u] = part
                pbuf[k * SLOTS + e + u] = both[u * BLK:(u + 1) * BLK, BLK:]
                top = jnp.max(fold(part), axis=0)
                m = top if m is None else jnp.maximum(m, top)
        m = jnp.broadcast_to(jnp.max(m, axis=0, keepdims=True), (8, BLK))
        yield True
        total = jnp.zeros((8, BLK), F32)
        dot = jnp.zeros((8, BLK), F32)
        for e in range(SLOTS):
            part = jnp.exp(fold(sbuf[k * SLOTS + e]) - m[None])
            sbuf[k * SLOTS + e] = part.reshape(BLK, BLK)
            total = total + jnp.sum(part, axis=0)
            dot = dot + jnp.sum(part * fold(pbuf[k * SLOTS + e]), axis=0)
        yield True
        inv = 1.0 / jnp.sum(total, axis=0, keepdims=True)
        delta = jnp.broadcast_to(jnp.sum(dot, axis=0, keepdims=True) * inv, (8, BLK))
        inv = jnp.broadcast_to(inv, (8, BLK))
        mixed = None
        for e, width in spans:
            pieces = []
            for u in range(width):
                prob = fold(sbuf[k * SLOTS + e + u]) * inv[None]
                ds = prob * (fold(pbuf[k * SLOTS + e + u]) - delta[None])
                pieces.append(jnp.concatenate(
                    [ds.reshape(BLK, BLK).astype(BF), prob.reshape(BLK, BLK).astype(BF)], axis=1))
            both = jnp.concatenate(pieces, axis=0)
            dkv = jnp.dot(both, qd2[k], preferred_element_type=F32)
            for u in range(width):
                parts[i * SLOTS + e + u] = dkv[u * BLK:(u + 1) * BLK].astype(BF)
            keys = jnp.concatenate([kvt_ref[slots[e + u]] for u in range(width)], axis=1)
            term = jnp.dot(keys, both, preferred_element_type=F32)
            term = (term[0:HDIM, 0:BLK], term[HDIM:, BLK:])
            mixed = term if mixed is None else (mixed[0] + term[0], mixed[1] + term[1])
        yield True
        od_ref[i] = jnp.concatenate([mixed[0] * 0.125, mixed[1]], axis=0).T.astype(BF)

    @pl.loop(0, HALF // 2)
    def _(t):
        i0 = 2 * ((mine // 2 - t + 8) % 8)
        for k in range(2):
            @pl.when(jnp.logical_not(is_self(i0 + k)))
            def _():
                qd_copy(i0 + k, i0 + k).wait_recv()

        @pl.when(t == 3)
        def _():
            @pl.loop(1, 4)
            def _(u):
                cot_across(x, (x + u) % 4).wait_recv()
                cot_beside((x + u) % 4, c).start()

        runs = [attend(i0 + k, k) for k in range(2)]
        while runs:
            runs = [run for run in runs if next(run, None)]
        for k in range(2):
            i = i0 + k

            @pl.when(jnp.logical_not(is_self(i)))
            def _():
                a_copy(i, mine).start()

            @pl.when(is_self(i))
            def _():
                ret_a[mine] = od_ref[i]

    def gathered(key):
        whole = None
        for i in range(HALF):
            part = parts[jnp.clip(table_s[key, 2 * i + c], 0, TILES)].astype(F32)
            whole = part if whole is None else whole + part
        return whole

    @pl.loop(0, 4)
    def _(t):
        r = (t + s // 8) % 4

        @pl.loop(0, 4)
        def _(u):
            j = r * 4 + u
            sib_out[j] = gathered(2 * j + 1 - c).astype(BF)

        s_copy(r).start()

    def back_chunk(t):
        r = (t + s // 8) % 4
        s_copy(r).wait_recv()

        @pl.loop(0, 4)
        def _(u):
            j = r * 4 + u
            send_b[j] = (gathered(2 * j + c) + sib[j].astype(F32)).astype(BF)

            @pl.when(jnp.logical_not(is_self(j)))
            def _():
                b_copy(j, mine).start()

            @pl.when(is_self(j))
            def _():
                ret_b[mine] = send_b[j]

    @pl.loop(0, HEADS // 2)
    def _(t):
        pair = (t + s // 4) % (HEADS // 2)
        cols = pl.ds(pl.multiple_of(pair * 128, 128), 128)
        for e in range(2):
            @pl.when(jnp.logical_not(is_self(pair * 2 + e)))
            def _():
                a_copy(pair * 2 + e, pair * 2 + e).wait_recv()

        a0 = ret_a[pair * 2]
        a1 = ret_a[pair * 2 + 1]
        at = jnp.concatenate([a0[:, 64:], a1[:, 64:]], axis=1)
        tiles[pair] = at

        @pl.when(pair != dp)
        def _():
            g_copy(pair, dp).start()

        @pl.when(pair == dp)
        def _():
            group[dp] = at

        flat[:, cols] = at

    back_chunk(0)

    cot_beside(x, 1 - c).wait_recv()

    @pl.loop(1, 4)
    def _(u):
        cot_beside((x + u) % 4, 1 - c).wait_recv()

    @pl.loop(0, SCENES)
    def _(p):
        @pl.when(p != dp)
        def _():
            g_copy(p, p).wait_recv()

    att = jnp.concatenate([group[p].T for p in range(SCENES)], axis=1)
    for q in range(4):
        grads = jnp.concatenate([cot_ref[p, :, q * 256:(q + 1) * 256] for p in range(SCENES)], axis=0)
        part = jnp.dot(att, grads, preferred_element_type=F32).astype(BF)
        for r in range(8):
            send_y[r * 4 + q] = part[r * 16:(r + 1) * 16]

    @pl.loop(1, 4)
    def _(t):
        y_copy((y + t) % 4, y).start()

    recv_y[y] = send_y[pl.ds(y * 8, 8)]

    back_chunk(1)

    @pl.loop(1, 4)
    def _(t):
        k = (y + 4 - t) % 4
        y_copy(k, k).wait_recv()

    for k in range(8):
        send_z[k] = (recv_y[0, k].astype(F32) + recv_y[1, k].astype(F32) + recv_y[2, k].astype(F32)
                     + recv_y[3, k].astype(F32)).astype(BF)

    @pl.loop(1, 8)
    def _(t):
        z_copy((z + t) % 8, z).start()

    recv_z[z] = send_z[z]
    back_chunk(2)

    @pl.loop(0, 4)
    def _(t):
        cols = pl.ds(pl.multiple_of(t * 256, 256), 256)
        o_ref[:, cols] = jnp.dot(flat[...], w_ref[:, cols], preferred_element_type=F32).astype(BF)

    @pl.loop(0, HEADS // 2)
    def _(pair):
        cols = pl.ds(pl.multiple_of(pair * 128, 128), 128)
        dq_ref[:, cols] = jnp.concatenate([ret_a[pair * 2][:, 0:64], ret_a[pair * 2 + 1][:, 0:64]], axis=1)

    @pl.loop(1, 8)
    def _(t):
        k = (z + 8 - t) % 8
        z_copy(k, k).wait_recv()

    whole = recv_z[0].astype(F32)
    for k in range(1, 8):
        whole = whole + recv_z[k].astype(F32)
    mine_w[...] = whole * (SCENES * NB * BLK) ** (-0.5)
    keeps = 4 * dp + s // 8 == s

    @pl.loop(0, SCENES)
    def _(t):
        p = (dp + t) % SCENES
        local_end = jnp.logical_and(t == 0, keeps)

        @pl.when(jnp.logical_not(local_end))
        def _():
            f_copy(p, s % 8).start()

        @pl.when(local_end)
        def _():
            stage[s % 8] = mine_w[...]

    back_chunk(3)

    @pl.loop(0, HEADS // 2)
    def _(pair):
        cols = pl.ds(pl.multiple_of(pair * 128, 128), 128)
        for e in range(2):
            @pl.when(jnp.logical_not(is_self(pair * 2 + e)))
            def _():
                b_copy(pair * 2 + e, pair * 2 + e).wait_recv()

        a0 = ret_b[pair * 2]
        a1 = ret_b[pair * 2 + 1]
        dk_ref[:, cols] = jnp.concatenate([a0[:, 0:64], a1[:, 0:64]], axis=1)
        dv_ref[:, cols] = jnp.concatenate([a0[:, 64:], a1[:, 64:]], axis=1)

    @pl.loop(0, SCENES)
    def _(t):
        @pl.when(jnp.logical_not(jnp.logical_and(s // 4 == dp, 8 * (s % 4) + t == s)))
        def _():
            f_copy(dp, t).wait_recv()

    for t in range(SCENES):
        wg_ref[16 * (t // 4):16 * (t // 4) + 16, 256 * (t % 4):256 * (t % 4) + 256] = stage[t]

    @pl.loop(0, HALF)
    def _(j):
        relay(j, c).wait_send()

        @pl.when(jnp.logical_not(is_self(j)))
        def _():
            kv_copy(j, s, mine).wait_send()
            qd_copy(j, mine).wait_send()
            a_copy(j, mine).wait_send()
            b_copy(j, mine).wait_send()

    @pl.loop(0, 4)
    def _(r):
        s_copy(r).wait_send()
        cot_beside(r, c).wait_send()

        @pl.when(r != x)
        def _():
            cot_across(r, x).wait_send()

    @pl.loop(0, SCENES)
    def _(t):
        p = (dp + t) % SCENES

        @pl.when(t != 0)
        def _():
            g_copy(p, dp).wait_send()

        @pl.when(jnp.logical_not(jnp.logical_and(t == 0, keeps)))
        def _():
            f_copy(p, s % 8).wait_send()

    @pl.loop(1, 4)
    def _(t):
        y_copy((y + t) % 4, y).wait_send()

    @pl.loop(1, 8)
    def _(t):
        z_copy((z + t) % 8, z).wait_send()


def local(node_queries, node_keys, node_values, cotangent, w_out, neighbours, contacts, ownership):
    flat = jax.ShapeDtypeStruct((BLK, DIM), BF)
    dma = pltpu.SemaphoreType.DMA
    rows = VMEM((BLK, DIM), BF)
    wide = lambda n, t=BF: VMEM((n, BLK, BLK), t)
    vmem = pl.BlockSpec(memory_space=VMEM)
    output, dq, dk, dv, weight_grad = pl.pallas_call(
        fused_kernel,
        out_shape=(flat,) * 4 + (jax.ShapeDtypeStruct((NB, DIM), F32),),
        in_specs=[pl.BlockSpec(memory_space=pltpu.HBM)] * 5 + [vmem] * 3,
        out_specs=(vmem,) * 5,
        scratch_shapes=[
            rows, rows, rows, VMEM((DIM, DIM), BF), VMEM((SCENES, BLK, DIM), BF),
            wide(HALF), wide(HALF), wide(NB), wide(NB), wide(HALF),
            VMEM((BLK, BLK), jnp.int32), VMEM((BLK, BLK), jnp.int32), VMEM((64, BLK), jnp.int32), pltpu.SMEM((64, BLK), jnp.int32),
            wide(2 * SLOTS, F32), wide(2 * SLOTS, F32), VMEM((2, 2 * BLK, BLK), BF), VMEM((2, BLK, 2 * BLK), BF),
            wide(TILES + 1), wide(HALF), wide(HALF),
            wide(HALF), wide(HALF), wide(HALF), wide(HALF), wide(SCENES), wide(SCENES), rows,
            VMEM((NB, 16, 256), BF), VMEM((4, 8, 16, 256), BF), VMEM((8, 16, 256), BF), VMEM((8, 16, 256), BF),
            VMEM((16, 256), F32), VMEM((SCENES, 16, 256), F32),
            dma((5,)), dma((HALF,)), dma((HALF,)), dma((HALF,)), dma((HALF,)), dma((HALF,)), dma((HALF,)), dma, dma, dma,
            dma((4,)), dma((4,)), dma((4,)), dma((4,)),
            dma((HALF,)), dma((HALF,)), dma((HALF,)), dma((HALF,)), dma((4,)), dma((4,)),
            dma((SCENES,)), dma((SCENES,)), dma((4,)), dma((4,)), dma((8,)), dma((8,)), dma((SCENES,)), dma((SCENES,)),
        ],
        compiler_params=pltpu.CompilerParams(
            collective_id=0, has_side_effects=True, vmem_limit_bytes=55259136),
        name="sublayer",
    )(node_queries[0], node_keys[0], node_values[0], cotangent[0], w_out, neighbours[0], contacts[0], ownership)
    return (output[None], dq[None], dk[None], dv[None], weight_grad)


def solution(mesh):
    placed = (
        P("dp", "seq", None), P("dp", "seq", None), P("dp", "seq", None), P("dp", "seq", None),
        P(), P("dp", None, None), P("dp", None, None), P("dp", None),
    )
    return jax.shard_map(
        local,
        mesh=mesh,
        in_specs=placed,
        out_specs=(
            P("dp", "seq", None), P("dp", "seq", None), P("dp", "seq", None), P("dp", "seq", None),
            P("seq", None),
        ),
        check_vma=False,
    )
```
